32 devices in a mesh: panel: 2 (over y), row: 4 (over z), layer: 4 (over x, core).
Axes of the slice: x: 2, y: 2, z: 4, core: 2. Of those that a mesh axis runs over, the one named last changes fastest.
Arguments:
- layers: bfloat16 [4, 8192, 512], P('layer', 'row', 'panel'), parts along dimension 2, may hold values from -6 to 6
- table: bfloat16 [16, 128, 64], replicated, may hold values from -0.375 to 0.375
- fitting: bfloat16 [8192, 6600], P('row', 'layer'), may hold values from -0.09375 to 0.09375
- owner: int32 [4, 128, 1], P('layer', 'row'), may hold values from 0 to 3; in each aligned block of 32 rows (0 to 31, 32 to 63, ..., all dimensions but the last counted through in order) at most 16 rows name the same one
- local_slice: int32 [4, 128], P('layer', 'row'), may hold values from 0 to 15
- block_index: int32 [4, 128], P('layer', 'row'), may hold values from 0 to 31
- weight_index: int32 [4, 128], P('layer', 'row'), may hold values from 0 to 15
Outputs:
- actuators: bfloat16 [512, 6600], P(('panel', 'row'), 'layer'), parts along dimension 0
The draws below stay inside these ranges and needn't reach their ends.
There are 2 independent parts, one for each index of `panel`. The reference program is written for one: setup_inputs(seed, part) draws one part's arguments, and reference() takes and returns one part's arrays. A program takes and returns all parts, laid end to end along the dimension named above; an argument that names none is the same for every part. Nothing has to cross between parts.
Inputs may be any that keep to these rules, and one draw needn't show every extreme that they name: `owner`: within the 32 entries of one layer on one row device (aligned blocks of 32 entries), no value is named more than 16 times, and in every draw some block names one value exactly 16 times.
All inputs are finite; a program needn't handle non-finite values.
Results may differ from the reference program's by a relative error of at most 0.0058.
Values may be sent and summed in bfloat16 or wider, within the bound.
No kernel may reach another device: no remote copies, remote signals or barrier semaphores. Data moves between devices by JAX's collectives and lax.ppermute only.
A program may use at most 64 MiB of HBM per device.

```python
import math
import jax
import jax.numpy as jnp
import numpy as np
from jax import lax

C = 256
NA = 6600
S = 128
B = 64
K = 16
SL_DEV = 16
E_DEV = 32
NL = 4
NP = 8192
NB = 32
NS = 64
NQ = 8192
ENT = 128
CAP = 16
N_ROW = 4


def touch_ends(result, rng, smallest, largest):
    place = [jax.random.randint(jax.random.fold_in(rng, axis), (), 0, length) for axis, length in enumerate(result.shape)]
    longest = result.shape.index(max(result.shape))
    beside = place[:longest] + [(place[longest] + 1) % result.shape[longest]] + place[longest + 1:]
    return result.at[tuple(place)].set(smallest).at[tuple(beside)].set(largest)


def raised(values, stream_key, source, target, parts, factor):
    def block_of(dim):
        return (jnp.arange(values.shape[dim]) // (values.shape[dim] // parts)).reshape((-1,) + (1,) * (values.ndim - 1 - dim))

    one_side = jax.random.permutation(stream_key, parts)[block_of(target)]
    other_side = (block_of(target) + parts // 2) % parts
    return jnp.where((block_of(source) == one_side) | (block_of(source) == other_side), factor * values, values)


def steps_of(key, shape, cuts, low, largest):
    loudness, own = 1.0, jax.random.fold_in(key, 6)
    for axis_at, shards_of in cuts:
        heights = jnp.exp(jax.random.uniform(jax.random.fold_in(own, axis_at), (shards_of,), jnp.float32, low / len(cuts), largest / len(cuts)))
        loudness = loudness * jnp.repeat(heights, shape[axis_at] // shards_of).reshape([-1 if axis == axis_at else 1 for axis in range(len(shape))])
    return loudness


def routed_block(key, own, number, rows, count, top, reach, slope):
    sequence = jax.random.permutation(key, count)
    crowded, common = load_shares(count, rows * top, reach, slope, True), load_shares(count, rows * top, reach, slope, False)
    places = jnp.arange(count)

    def named(sizes, turn):
        used = int((sizes > 0).sum())
        fixed = max(1, used // 4)
        passed = fixed + (places - fixed + turn * (used - fixed)) % max(1, count - fixed)
        return jnp.zeros((count,), jnp.int32).at[sequence[jnp.where(places < fixed, places, passed)]].set(jnp.asarray(sizes, jnp.int32))

    sizes = jnp.where(number % 4 == 0, named(crowded, number // 4), named(common, number - number // 4 - 1))
    mixed = jax.random.permutation(jax.random.fold_in(own, 3), count)
    source_of, receiver = mixed[0:count // 2 * 2:2], mixed[1:count // 2 * 2:2]
    slack = jnp.minimum(sizes[source_of] - 1, reach - sizes[receiver]) // 2
    slack = jnp.where((source_of == sequence[0]) | (receiver == sequence[0]) | (sizes[receiver] == 0), 0, jnp.maximum(slack, 0))
    passed = jax.random.randint(jax.random.fold_in(own, 4), (count // 2,), 0, 1 << 20) % (slack + 1)
    sizes = sizes.at[source_of].add(-passed).at[receiver].add(passed)
    labels = jnp.searchsorted(jnp.cumsum(sizes), jnp.arange(rows * top), side="right").astype(jnp.int32)
    grid = labels.reshape(top, rows).T
    grid = grid[jax.random.permutation(jax.random.fold_in(own, 1), rows)]
    turn = jax.random.randint(jax.random.fold_in(own, 2), (rows, 1), 0, top)
    return jnp.take_along_axis(grid, (jnp.arange(top)[None, :] + turn) % top, axis=1)


def load_shares(amount, total, most, slope, full):
    loads = [(1 << 20) // math.isqrt(grade ** slope) + 1 for grade in range(1, amount + 1)]
    largest = most if full else min(most, max(-(-total // amount), total * loads[0] // sum(loads)))
    least = 1 if total - largest >= amount - 1 else 0
    holding, rest = [largest] + [least] * (amount - 1), total - largest - least * (amount - 1)
    while rest > 0:
        movable = [i for i in range(1, amount) if holding[i] < largest] or [i for i in range(1, amount) if holding[i] < most]
        pool, left = sum([loads[i] for i in movable]), rest
        for i in movable:
            extra = min(most - holding[i], max(1, left * loads[i] // pool), rest)
            holding[i] = holding[i] + extra
            rest = rest - extra
    return np.array(holding)


def centred(stream_key, shape, deviation, most, pieces=(), kind=jnp.bfloat16):
    loudness = steps_of(stream_key, shape, pieces, -0.22, 0.18) if pieces else 1.0
    drawn = jax.random.normal(stream_key, shape, jnp.float32) * deviation * loudness
    return jnp.minimum(jnp.maximum(drawn, -most), most).astype(kind)


def gaussian_with(key, dims, width, limit, pieces, heavy, held_as=jnp.bfloat16):
    values = width * jax.random.normal(key, dims, jnp.float32)
    if pieces:
        values = values * steps_of(key, dims, pieces, -0.22, 0.18)
    return jnp.clip(raised(values, jax.random.fold_in(key, 3), *heavy), -limit, limit).astype(held_as)


def setup_inputs(seed: int = 0, part: int = 0) -> dict:
    splits = jax.random.split(jax.random.key(seed), 8)
    part_keys = jax.random.split(jax.random.fold_in(splits[7], part), 8)
    layers = centred(part_keys[0], (NL, NP, C), 1.0, 6.0, ((0, 4), (1, 4)))
    table = centred(splits[1], (K, S, B), (4 * B) ** -0.5, 0.375)
    fitting = gaussian_with(splits[2], (NQ, NA), NQ ** -0.5, 0.09375, ((0, 4), (1, 4)), (0, 1, 4, 2.0))
    owner_keys = jax.random.split(jax.random.fold_in(splits[3], 1), NL * ENT // E_DEV)
    owner_turns = jax.random.permutation(jax.random.fold_in(splits[3], 3), NL * ENT // E_DEV)
    owner = jax.vmap(lambda own, number: routed_block(jax.random.fold_in(splits[3], 2), own, number, E_DEV, N_ROW, 1, CAP, 2))(owner_keys, owner_turns).reshape((NL, ENT, 1))
    local_slice = touch_ends(jax.random.randint(splits[4], (NL, ENT), 0, SL_DEV), jax.random.fold_in(splits[4], 1), 0, SL_DEV - 1).astype(jnp.int32)
    block_index = touch_ends(jax.random.randint(splits[5], (NL, ENT), 0, NB), jax.random.fold_in(splits[5], 1), 0, NB - 1).astype(jnp.int32)
    weight_index = touch_ends(jax.random.randint(splits[6], (NL, ENT), 0, K), jax.random.fold_in(splits[6], 1), 0, K - 1).astype(jnp.int32)
    return {"layers": layers, "table": table, "fitting": fitting, "owner": owner, "local_slice": local_slice, "block_index": block_index, "weight_index": weight_index}


def reference(layers, table, fitting, owner, local_slice, block_index, weight_index):
    layer_total = layers.shape[0]

    def one_layer(running, layer_index):
        layer_rows = lax.dynamic_index_in_dim(layers, layer_index, 0, keepdims=False)
        owner_now = lax.dynamic_index_in_dim(owner, layer_index, 0, keepdims=False)[:, 0]
        local_now = lax.dynamic_index_in_dim(local_slice, layer_index, 0, keepdims=False)
        block_now = lax.dynamic_index_in_dim(block_index, layer_index, 0, keepdims=False)
        weight_now = lax.dynamic_index_in_dim(weight_index, layer_index, 0, keepdims=False)
        source_dev = (jnp.arange(ENT, dtype=jnp.int32) // E_DEV).astype(jnp.int32)
        start_block = (source_dev * NB + block_now).astype(jnp.int32)
        grouped = layer_rows.reshape(NB * N_ROW, B, C)
        picked = grouped[start_block].astype(jnp.float32)
        weights = table[weight_now].astype(jnp.float32)
        term = jnp.einsum("esb,ebc->esc", weights, picked).astype(jnp.bfloat16)
        destination = (owner_now * SL_DEV + local_now).astype(jnp.int32)
        running = running + jax.ops.segment_sum(term.astype(jnp.float32), destination, num_segments=NS)
        return running, None

    pupil, _ = lax.scan(one_layer, jnp.zeros((NS, S, C), jnp.float32), jnp.arange(layer_total, dtype=jnp.int32))
    pupil_rounded = pupil.reshape(NQ, C).astype(jnp.bfloat16)
    return jnp.dot(pupil_rounded.T, fitting, preferred_element_type=jnp.float32).astype(jnp.bfloat16)
```

```python
import functools

import jax
import jax.numpy as jnp
from jax import lax
from jax.experimental import pallas as pl
from jax.experimental.pallas import tpu as pltpu
from jax.sharding import PartitionSpec as P

LANES = 128
F32, BF16 = jnp.float32, jnp.bfloat16
VMEM = pl.BlockSpec(memory_space=pltpu.VMEM)
SMEM = pl.BlockSpec(memory_space=pltpu.SMEM)
PARAMS = dict(vmem_limit_bytes=48 * 1024 * 1024)


def turn_kernel(layers_ref, *outs):
    columns = layers_ref.shape[1]
    each = outs[0].shape[0]
    first = lax.axis_index("layer") * each
    row = lax.broadcasted_iota(jnp.int32, (columns, columns), 0)
    col = lax.broadcasted_iota(jnp.int32, (columns, columns), 1)
    pick = (col == lax.rem(row + first, columns)).astype(BF16)
    turned = lax.dot_general(
        pick, layers_ref[...], (((1,), (1,)), ((), ())), preferred_element_type=F32
    ).astype(BF16)
    for k, out in enumerate(outs):
        out[...] = turned[k * each : (k + 1) * each]


def pupil_kernel(n_layer, n_row, unroll, table_ref, *refs):
    codes, parts = refs[:n_layer], refs[n_layer : 2 * n_layer]
    outs, total = refs[2 * n_layer : 2 * n_layer + n_row], refs[-1]
    weights = table_ref.shape[0] // 2
    owned = outs[0].shape[1] // LANES
    total[...] = jnp.zeros_like(total)
    for code, part in zip(codes, parts):

        def step(group, carry):
            terms = []
            for u in range(unroll):
                e = group * unroll + u
                block = code[1, e]
                source = part[:, pl.ds(pl.multiple_of((block // 2) * LANES, LANES), LANES)]
                weight = table_ref[lax.rem(block, 2) * weights + code[2, e]]
                terms.append((code[0, e], jnp.dot(source, weight, preferred_element_type=F32)))
            for dest, term in terms:
                total[dest] += term
            return carry

        lax.fori_loop(0, code.shape[1] // unroll, step, 0)
    me = lax.axis_index("row")
    for k, out in enumerate(outs):
        base = lax.rem(me + k, n_row) * owned
        for s in range(owned):
            out[:, s * LANES : (s + 1) * LANES] = total[base + s].astype(BF16)


def fit_kernel(n_layer, n_row, fitting_ref, *refs):
    pieces, outs = refs[:n_layer], refs[n_layer : n_layer + n_row]
    left, product = refs[-2], refs[-1]

    @pl.when(pl.program_id(0) == 0)
    def _():
        me = lax.axis_index("layer")
        for j, piece in enumerate(pieces):
            left[lax.rem(me + n_layer - j, n_layer)] = piece[...]

    columns = product.shape[0]
    product[...] = jnp.dot(
        left[...].reshape(columns, left.shape[2]), fitting_ref[...], preferred_element_type=F32
    )
    each = columns // n_row
    me = lax.axis_index("row")
    for k, out in enumerate(outs):
        start = pl.multiple_of(lax.rem(me + k, n_row) * each, each)
        out[...] = product[pl.ds(start, each), :].astype(BF16)


def exchange(chunks, axis):
    n = len(chunks)
    return [
        chunk if k == 0 else lax.ppermute(chunk, axis, [(i, (i + k) % n) for i in range(n)])
        for k, chunk in enumerate(chunks)
    ]


def total_of(parts):
    return sum(part.astype(F32) for part in parts).astype(BF16)


def local(layers, table, fitting, owner, local_slice, block_index, weight_index):
    n_layer, n_row = lax.axis_size("layer"), lax.axis_size("row")
    rows_dev, columns = layers.shape[1:]
    weights, slice_rows, block_rows = table.shape
    points, actuators = fitting.shape
    owned = points // slice_rows
    each = columns // n_layer

    dest = owner[0, :, 0] * owned + local_slice[0]
    code = jnp.stack([dest, block_index[0], weight_index[0]])
    codes = exchange([code] * n_layer, "layer")

    turned = pl.pallas_call(
        turn_kernel,
        out_shape=[jax.ShapeDtypeStruct((each, rows_dev), BF16)] * n_layer,
        in_specs=[VMEM],
        out_specs=[VMEM] * n_layer,
        compiler_params=pltpu.CompilerParams(**PARAMS),
    )(layers[0])
    parts = exchange(turned, "layer")

    flipped = jnp.swapaxes(table, 1, 2)
    nothing = jnp.zeros_like(flipped)
    padded = jnp.concatenate(
        [jnp.concatenate([flipped, nothing], 1), jnp.concatenate([nothing, flipped], 1)], 0
    )
    shares = pl.pallas_call(
        functools.partial(pupil_kernel, n_layer, n_row, 8),
        out_shape=[jax.ShapeDtypeStruct((each, points), BF16)] * n_row,
        in_specs=[VMEM] + [SMEM] * n_layer + [VMEM] * n_layer,
        out_specs=[VMEM] * n_row,
        scratch_shapes=[pltpu.VMEM((n_row * owned, each, slice_rows), F32)],
        compiler_params=pltpu.CompilerParams(**PARAMS),
    )(padded, *codes, *parts)
    pupil = total_of(exchange(shares, "row"))
    pieces = exchange([pupil] * n_layer, "layer")

    tile = 2 * LANES
    partial = pl.pallas_call(
        functools.partial(fit_kernel, n_layer, n_row),
        grid=(pl.cdiv(actuators, tile),),
        out_shape=[jax.ShapeDtypeStruct((columns // n_row, actuators), BF16)] * n_row,
        in_specs=[pl.BlockSpec((points, tile), lambda i: (0, i))] + [VMEM] * n_layer,
        out_specs=[pl.BlockSpec((columns // n_row, tile), lambda i: (0, i))] * n_row,
        scratch_shapes=[
            pltpu.VMEM((n_layer, each, points), BF16),
            pltpu.VMEM((columns, tile), F32),
        ],
        compiler_params=pltpu.CompilerParams(**PARAMS),
    )(fitting, *pieces)
    return total_of(exchange(partial, "row"))


def solution(mesh):
    return jax.shard_map(
        local,
        mesh=mesh,
        in_specs=(
            P("layer", "row", "panel"),
            P(),
            P("row", "layer"),
            P("layer", "row", None),
            P("layer", "row"),
            P("layer", "row"),
            P("layer", "row"),
        ),
        out_specs=P(("panel", "row"), "layer"),
        check_vma=False,
    )
```

```python
import functools

import jax
import jax.numpy as jnp
from jax import lax
from jax.experimental import pallas as pl
from jax.experimental.pallas import tpu as pltpu
from jax.sharding import PartitionSpec as P

LANES = 128
CODE_ROWS = 16
F32, BF16 = jnp.float32, jnp.bfloat16
VMEM = pl.BlockSpec(memory_space=pltpu.VMEM)
HBM = pl.BlockSpec(memory_space=pltpu.HBM)
PARAMS = dict(vmem_limit_bytes=48 * 1024 * 1024)


def turn_kernel(n_layer, n_row, halves, layers_hbm, *refs):
    index_refs, outs, near, (layers_ref, codes, sems) = refs[:4], refs[4:-7], refs[-7:-3], refs[-3:]
    loads = [pltpu.make_async_copy(layers_hbm, layers_ref, sems.at[4])]
    loads[0].start()
    rows_dev, columns = layers_ref.shape
    per_half = columns // halves
    each = per_half // n_layer
    chunk, part = columns // n_row, columns // n_row // halves
    codes[...] = jnp.zeros_like(codes)
    for i, ref in enumerate(index_refs):
        loads.append(pltpu.make_async_copy(ref, near[i], sems.at[i]))
        loads[-1].start()
    first = lax.axis_index("layer") * each
    row = lax.broadcasted_iota(jnp.int32, (per_half, columns), 0)
    col = lax.broadcasted_iota(jnp.int32, (per_half, columns), 1)
    place = lax.rem(row + first, per_half)
    wanted = (place // part) * chunk + lax.rem(place, part)
    for load in loads:
        load.wait()
    for i, ref in enumerate(near):
        codes[i : i + 1, : ref.shape[1]] = ref[...]
    tail = codes[...].astype(F32).astype(BF16)
    for h in range(halves):
        pick = (col == wanted + h * part).astype(BF16)
        turned = lax.dot_general(
            pick, layers_ref[...], (((1,), (1,)), ((), ())), preferred_element_type=F32
        ).astype(BF16)
        for k in range(n_layer):
            out = outs[h * n_layer + k]
            out[:, :rows_dev] = turned[k * each : (k + 1) * each]
            if h == 0:
                out[:, rows_dev:] = jnp.zeros((each, LANES), BF16)
                out[:CODE_ROWS, rows_dev:] = tail


def pupil_kernel(n_layer, n_row, entries, unroll, table_ref, *refs):
    coded, parts = refs[:n_layer], refs[n_layer : 2 * n_layer]
    outs = refs[2 * n_layer : 2 * n_layer + n_row]
    total, codes, code, sem = refs[-4:]
    weights = table_ref.shape[0] // 2
    owned = outs[0].shape[1] // LANES
    for j, ref in enumerate(coded):
        tail = ref[:CODE_ROWS, ref.shape[1] - LANES :]
        codes[j * CODE_ROWS : (j + 1) * CODE_ROWS] = tail.astype(F32).astype(jnp.int32)
    copy = pltpu.make_async_copy(codes, code, sem)
    copy.start()
    total[...] = jnp.zeros_like(total)
    copy.wait()
    for j, part in enumerate(parts):
        base = j * CODE_ROWS

        def step(group, carry):
            terms = []
            for u in range(unroll):
                e = group * unroll + u
                block = code[base + 2, e]
                source = part[:, pl.ds(pl.multiple_of((block // 2) * LANES, LANES), LANES)]
                weight = table_ref[lax.rem(block, 2) * weights + code[base + 3, e]]
                dest = code[base, e] * owned + code[base + 1, e]
                terms.append((dest, jnp.dot(source, weight, preferred_element_type=F32)))
            for dest, term in terms:
                total[dest] += term
            return carry

        lax.fori_loop(0, entries // unroll, step, 0)
    me = lax.axis_index("row")
    for k, out in enumerate(outs):
        base = lax.rem(me + k, n_row) * owned
        for s in range(owned):
            out[:, s * LANES : (s + 1) * LANES] = total[base + s].astype(BF16)


def ready_kernel(table_ref, fitting_hbm, padded_ref, fitting_ref, sem):
    load = pltpu.make_async_copy(fitting_hbm, fitting_ref, sem)
    load.start()
    weights, block_rows = table_ref.shape[:2]
    padded_ref[...] = jnp.zeros_like(padded_ref)
    for half in range(LANES // block_rows):
        for w in range(weights):
            padded_ref[half * weights + w, half * block_rows : (half + 1) * block_rows] = table_ref[w]
    load.wait()


def fit_kernel(n_layer, n_row, fitting_ref, *refs):
    pieces, outs = refs[:n_layer], refs[n_layer : n_layer + n_row]
    left, product = refs[-2], refs[-1]
    aligned = n_layer == n_row
    me, row = lax.axis_index("layer"), lax.axis_index("row")
    for j, piece in enumerate(pieces):
        place = me + n_layer - j
        left[lax.rem(place + n_row - row if aligned else place, n_layer)] = piece[...]
    columns = left.shape[0] * left.shape[1]
    found = lax.dot_general(
        left[...].reshape(columns, left.shape[2]),
        fitting_ref[...],
        (((1,), (1,)), ((), ())),
        preferred_element_type=F32,
    )
    each = columns // n_row
    if aligned:
        for k, out in enumerate(outs):
            out[...] = found[k * each : (k + 1) * each].astype(BF16)
    else:
        product[...] = found
        for k, out in enumerate(outs):
            start = pl.multiple_of(lax.rem(row + k, n_row) * each, each)
            out[...] = product[pl.ds(start, each), :].astype(BF16)


def exchange(chunks, axis):
    n = len(chunks)
    return [
        chunk if k == 0 else lax.ppermute(chunk, axis, [(i, (i + k) % n) for i in range(n)])
        for k, chunk in enumerate(chunks)
    ]


def total_of(parts):
    return sum(part.astype(F32) for part in parts).astype(BF16)


def call(kernel, micros, shapes, scratch, *args, far=()):
    return pl.pallas_call(
        kernel,
        out_shape=[jax.ShapeDtypeStruct(shape, BF16) for shape in shapes],
        in_specs=[HBM if i in far else VMEM for i in range(len(args))],
        out_specs=[VMEM] * len(shapes),
        scratch_shapes=scratch,
        cost_estimate=pl.CostEstimate(
            flops=0, transcendentals=0, bytes_accessed=int(micros * 3.69e6)
        ),
        compiler_params=pltpu.CompilerParams(**PARAMS),
    )(*args)


def local(layers, table, fitting, owner, local_slice, block_index, weight_index):
    n_layer, n_row = lax.axis_size("layer"), lax.axis_size("row")
    rows_dev, columns = layers.shape[1:]
    entries = owner.shape[1]
    weights, slice_rows, block_rows = table.shape
    points, actuators = fitting.shape
    owned = points // slice_rows
    chunk = columns // n_row
    halves = 2 if chunk % 32 == 0 else 1
    per_half = columns // halves
    each = per_half // n_layer

    turned = call(
        functools.partial(turn_kernel, n_layer, n_row, halves),
        2,
        [(each, rows_dev + (LANES if h == 0 else 0)) for h in range(halves) for _ in range(n_layer)],
        [pltpu.VMEM((1, entries), jnp.int32)] * 4
        + [
            pltpu.VMEM((rows_dev, columns), BF16),
            pltpu.VMEM((CODE_ROWS, LANES), jnp.int32),
            pltpu.SemaphoreType.DMA((5,)),
        ],
        layers[0],
        owner[:, :, 0],
        local_slice,
        block_index,
        weight_index,
        far=range(5),
    )
    padded, held = call(
        ready_kernel,
        2,
        [(LANES // block_rows * weights, LANES, slice_rows), (actuators, points)],
        [pltpu.SemaphoreType.DMA],
        jnp.swapaxes(table, 1, 2),
        fitting.T,
        far=(1,),
    )
    parts = []
    for h in range(halves):
        sent = turned[h * n_layer : (h + 1) * n_layer]
        if h > 0:
            sent, parts[-1] = lax.optimization_barrier((sent, parts[-1]))
        parts.append(exchange(sent, "layer"))
    received = []
    for h in range(halves):
        shares = call(
            functools.partial(pupil_kernel, n_layer, n_row, entries, 8),
            4,
            [(each, points)] * n_row,
            [
                pltpu.VMEM((n_row * owned, each, slice_rows), F32),
                pltpu.VMEM((n_layer * CODE_ROWS, LANES), jnp.int32),
                pltpu.SMEM((n_layer * CODE_ROWS, LANES), jnp.int32),
                pltpu.SemaphoreType.DMA,
            ],
            padded,
            *parts[0],
            *parts[h],
        )
        received.append(exchange(shares, "row"))
    results = []
    for h in range(halves):
        pieces = exchange([total_of(received[h])] * n_layer, "layer")
        partial = call(
            functools.partial(fit_kernel, n_layer, n_row),
            4,
            [(chunk // halves, actuators)] * n_row,
            [pltpu.VMEM((n_layer, each, points), BF16), pltpu.VMEM((per_half, actuators), F32)],
            held,
            *pieces,
        )
        results.append(exchange(partial, "row"))
    return jnp.concatenate([total_of(result) for result in results], 0)


def solution(mesh):
    return jax.shard_map(
        local,
        mesh=mesh,
        in_specs=(
            P("layer", "row", "panel"),
            P(),
            P("row", "layer"),
            P("layer", "row", None),
            P("layer", "row"),
            P("layer", "row"),
            P("layer", "row"),
        ),
        out_specs=P(("panel", "row"), "layer"),
        check_vma=False,
    )
```

```python
import functools

import jax
import jax.numpy as jnp
from jax import lax
from jax.experimental import pallas as pl
from jax.experimental.pallas import tpu as pltpu
from jax.sharding import PartitionSpec as P

LANES = 128
CODE_ROWS = 16
F32, BF16 = jnp.float32, jnp.bfloat16
VMEM = pl.BlockSpec(memory_space=pltpu.VMEM)
ANY = pl.BlockSpec(memory_space=pl.ANY)
PARAMS = dict(vmem_limit_bytes=16 * 1024 * 1024)


def turn_kernel(n_layer, n_row, halves, layers_ref, tail_ref, *outs):
    rows_dev, columns = layers_ref.shape
    per_half = columns // halves
    each = per_half // n_layer
    chunk, part = columns // n_row, columns // n_row // halves
    first = lax.axis_index("layer") * each
    row = lax.broadcasted_iota(jnp.int32, (per_half, columns), 0)
    col = lax.broadcasted_iota(jnp.int32, (per_half, columns), 1)
    place = lax.rem(row + first, per_half)
    wanted = (place // part) * chunk + lax.rem(place, part)
    for h in range(halves):
        pick = (col == wanted + h * part).astype(BF16)
        turned = lax.dot_general(
            pick, layers_ref[...], (((1,), (1,)), ((), ())), preferred_element_type=F32
        ).astype(BF16)
        for k in range(n_layer):
            out = outs[h * n_layer + k]
            out[:, :rows_dev] = turned[k * each : (k + 1) * each]
            if h == 0:
                out[:, rows_dev:] = jnp.zeros((each, LANES), BF16)
                out[:CODE_ROWS, rows_dev:] = tail_ref[...]


def pupil_kernel(n_layer, n_row, entries, unroll, table_ref, *refs):
    coded, parts = refs[:n_layer], refs[n_layer : 2 * n_layer]
    outs = refs[2 * n_layer : 2 * n_layer + n_row]
    total, codes, code, sem = refs[-4:]
    weights = table_ref.shape[0] // 2
    owned = outs[0].shape[1] // LANES
    for j, ref in enumerate(coded):
        tail = ref[:CODE_ROWS, ref.shape[1] - LANES :]
        codes[j * CODE_ROWS : (j + 1) * CODE_ROWS] = tail.astype(F32).astype(jnp.int32)
    copy = pltpu.make_async_copy(codes, code, sem)
    copy.start()
    total[...] = jnp.zeros_like(total)
    copy.wait()
    for j, part in enumerate(parts):
        base = j * CODE_ROWS

        def step(group, carry):
            terms = []
            for u in range(unroll):
                e = group * unroll + u
                block = code[base + 2, e]
                source = part[:, pl.ds(pl.multiple_of((block // 2) * LANES, LANES), LANES)]
                weight = table_ref[lax.rem(block, 2) * weights + code[base + 3, e]]
                dest = code[base, e] * owned + code[base + 1, e]
                terms.append((dest, jnp.dot(source, weight, preferred_element_type=F32)))
            for dest, term in terms:
                total[dest] += term
            return carry

        lax.fori_loop(0, entries // unroll, step, 0)
    me = lax.axis_index("row")
    for k, out in enumerate(outs):
        base = lax.rem(me + k, n_row) * owned
        for s in range(owned):
            out[:, s * LANES : (s + 1) * LANES] = total[base + s].astype(BF16)


def sum_kernel(*refs):
    refs[-1][...] = sum(ref[...].astype(F32) for ref in refs[:-1]).astype(BF16)


def fit_kernel(n_layer, n_row, fitting_ref, *refs):
    pieces, outs = refs[:n_layer], refs[n_layer : n_layer + n_row]
    left, product = refs[-2], refs[-1]
    aligned = n_layer == n_row
    me, row = lax.axis_index("layer"), lax.axis_index("row")
    for j, piece in enumerate(pieces):
        place = me + n_layer - j
        left[lax.rem(place + n_row - row if aligned else place, n_layer)] = piece[...]
    columns = left.shape[0] * left.shape[1]
    found = lax.dot_general(
        left[...].reshape(columns, left.shape[2]),
        fitting_ref[...],
        (((1,), (1,)), ((), ())),
        preferred_element_type=F32,
    )
    each = columns // n_row
    if aligned:
        for k, out in enumerate(outs):
            out[...] = found[k * each : (k + 1) * each].astype(BF16)
    else:
        product[...] = found
        for k, out in enumerate(outs):
            start = pl.multiple_of(lax.rem(row + k, n_row) * each, each)
            out[...] = product[pl.ds(start, each), :].astype(BF16)


def exchange(chunks, axis):
    n = len(chunks)
    return [
        chunk if k == 0 else lax.ppermute(chunk, axis, [(i, (i + k) % n) for i in range(n)])
        for k, chunk in enumerate(chunks)
    ]


def total_of(parts):
    return sum(part.astype(F32) for part in parts).astype(BF16)


def call(kernel, shapes, scratch, *args, after=()):
    def body(*refs):
        kernel(*refs[: len(args)], *refs[len(args) + len(after) :])

    return pl.pallas_call(
        body,
        out_shape=[jax.ShapeDtypeStruct(shape, BF16) for shape in shapes],
        in_specs=[VMEM] * len(args) + [ANY] * len(after),
        out_specs=[VMEM] * len(shapes),
        scratch_shapes=scratch,
        compiler_params=pltpu.CompilerParams(**PARAMS),
    )(*args, *after)


def local(layers, table, fitting, owner, local_slice, block_index, weight_index):
    n_layer, n_row = lax.axis_size("layer"), lax.axis_size("row")
    rows_dev, columns = layers.shape[1:]
    entries = owner.shape[1]
    weights, slice_rows, block_rows = table.shape
    points, actuators = fitting.shape
    owned = points // slice_rows
    chunk = columns // n_row
    halves = 2 if chunk % 32 == 0 else 1
    per_half = columns // halves
    each = per_half // n_layer

    tail = jnp.concatenate([owner[:, :, 0], local_slice, block_index, weight_index], 0)
    tail = jnp.pad(tail.astype(BF16), ((0, CODE_ROWS - 4), (0, LANES - entries)))
    turned = call(
        functools.partial(turn_kernel, n_layer, n_row, halves),
        [(each, rows_dev + (LANES if h == 0 else 0)) for h in range(halves) for _ in range(n_layer)],
        [],
        layers[0],
        tail,
    )
    parts = []
    for h in range(halves):
        sent = turned[h * n_layer : (h + 1) * n_layer]
        if h > 0:
            sent, parts[-1] = lax.optimization_barrier((sent, parts[-1]))
        parts.append(exchange(sent, "layer"))

    flipped = jnp.swapaxes(table, 1, 2)
    nothing = jnp.zeros_like(flipped)
    padded = jnp.concatenate(
        [jnp.concatenate([flipped, nothing], 1), jnp.concatenate([nothing, flipped], 1)], 0
    )
    received, before = [], ()
    for h in range(halves):
        shares = call(
            functools.partial(pupil_kernel, n_layer, n_row, entries, entries),
            [(each, points)] * n_row,
            [
                pltpu.VMEM((n_row * owned, each, slice_rows), F32),
                pltpu.VMEM((n_layer * CODE_ROWS, LANES), jnp.int32),
                pltpu.SMEM((n_layer * CODE_ROWS, LANES), jnp.int32),
                pltpu.SemaphoreType.DMA,
            ],
            padded,
            *parts[0],
            *parts[h],
            after=before,
        )
        before = (shares[0],)
        received.append(exchange(shares, "row"))
    results = []
    for h in range(halves):
        (pupil,) = call(sum_kernel, [(each, points)], [], *received[h], after=before)
        pieces = exchange([pupil] * n_layer, "layer")
        partial = call(
            functools.partial(fit_kernel, n_layer, n_row),
            [(chunk // halves, actuators)] * n_row,
            [pltpu.VMEM((n_layer, each, points), BF16), pltpu.VMEM((per_half, actuators), F32)],
            fitting.T,
            *pieces,
        )
        before = (partial[0],)
        results.append(exchange(partial, "row"))
    return jnp.concatenate([total_of(result) for result in results], 0)


def solution(mesh):
    return jax.shard_map(
        local,
        mesh=mesh,
        in_specs=(
            P("layer", "row", "panel"),
            P(),
            P("row", "layer"),
            P("layer", "row", None),
            P("layer", "row"),
            P("layer", "row"),
            P("layer", "row"),
        ),
        out_specs=P(("panel", "row"), "layer"),
        check_vma=False,
    )
```

```python
import functools

import jax
import jax.numpy as jnp
from jax import lax
from jax.experimental import pallas as pl
from jax.experimental.pallas import tpu as pltpu
from jax.sharding import PartitionSpec as P

LANES = 128
CODE_ROWS = 16
F32, BF16 = jnp.float32, jnp.bfloat16
VMEM = pl.BlockSpec(memory_space=pltpu.VMEM)
ANY = pl.BlockSpec(memory_space=pl.ANY)
PARAMS = dict(vmem_limit_bytes=16 * 1024 * 1024)


def turn_kernel(n_layer, n_row, halves, half, layers_ref, extra_ref, *refs):
    outs, codes = refs[:n_layer], refs[-1]
    rows_dev, columns = layers_ref.shape
    per_half = columns // halves
    each = per_half // n_layer
    chunk, part = columns // n_row, columns // n_row // halves
    first = lax.axis_index("layer") * each
    row = lax.broadcasted_iota(jnp.int32, (per_half, columns), 0)
    col = lax.broadcasted_iota(jnp.int32, (per_half, columns), 1)
    place = lax.rem(row + first, per_half)
    wanted = (place // part) * chunk + lax.rem(place, part) + half * part
    pick = (col == wanted).astype(BF16)
    turned = lax.dot_general(
        pick, layers_ref[...], (((1,), (1,)), ((), ())), preferred_element_type=F32
    ).astype(BF16)
    for k, out in enumerate(outs):
        out[:, :rows_dev] = turned[k * each : (k + 1) * each]
    if half == 0:
        codes[...] = jnp.zeros_like(codes)
        codes[: extra_ref.shape[0], : extra_ref.shape[1]] = extra_ref[...]
        tail = codes[...].astype(F32).astype(BF16)
        for out in outs:
            out[:, rows_dev:] = jnp.zeros((each, LANES), BF16)
            out[:CODE_ROWS, rows_dev:] = tail


def pad_kernel(table_ref, padded):
    weights, block_rows = table_ref.shape[:2]
    padded[...] = jnp.zeros_like(padded)
    for half in range(LANES // block_rows):
        start = half * block_rows
        padded[half * weights : (half + 1) * weights, start : start + block_rows] = table_ref[...]


def pupil_kernel(n_layer, n_row, entries, unroll, padded, *refs):
    coded, parts = refs[:n_layer], refs[n_layer : 2 * n_layer]
    outs = refs[2 * n_layer : 2 * n_layer + n_row]
    total, codes, code, sem = refs[-4:]
    weights = padded.shape[0] // 2
    owned = outs[0].shape[1] // LANES
    for j, ref in enumerate(coded):
        tail = ref[:CODE_ROWS, ref.shape[1] - LANES :]
        codes[j * CODE_ROWS : (j + 1) * CODE_ROWS] = tail.astype(F32).astype(jnp.int32)
    copy = pltpu.make_async_copy(codes, code, sem)
    copy.start()
    total[...] = jnp.zeros_like(total)
    copy.wait()
    for j, part in enumerate(parts):
        base = j * CODE_ROWS

        def step(group, carry):
            terms = []
            for u in range(unroll):
                e = group * unroll + u
                block = code[base + 2, e]
                source = part[:, pl.ds(pl.multiple_of((block // 2) * LANES, LANES), LANES)]
                weight = padded[lax.rem(block, 2) * weights + code[base + 3, e]]
                dest = code[base, e] * owned + code[base + 1, e]
                terms.append((dest, jnp.dot(source, weight, preferred_element_type=F32)))
            for dest, term in terms:
                total[dest] += term
            return carry

        lax.fori_loop(0, entries // unroll, step, 0)
    me = lax.axis_index("row")
    for k, out in enumerate(outs):
        base = lax.rem(me + k, n_row) * owned
        for s in range(owned):
            out[:, s * LANES : (s + 1) * LANES] = total[base + s].astype(BF16)


def sum_kernel(*refs):
    refs[-1][...] = sum(ref[...].astype(F32) for ref in refs[:-1]).astype(BF16)


def fit_kernel(n_layer, n_row, fitting_ref, *refs):
    pieces, outs = refs[:n_layer], refs[n_layer : n_layer + n_row]
    left, product = refs[-2], refs[-1]
    aligned = n_layer == n_row
    me, row = lax.axis_index("layer"), lax.axis_index("row")
    for j, piece in enumerate(pieces):
        place = me + n_layer - j
        left[lax.rem(place + n_row - row if aligned else place, n_layer)] = piece[...]
    columns = left.shape[0] * left.shape[1]
    found = lax.dot_general(
        left[...].reshape(columns, left.shape[2]),
        fitting_ref[...],
        (((1,), (1,)), ((), ())),
        preferred_element_type=F32,
    )
    each = columns // n_row
    if aligned:
        for k, out in enumerate(outs):
            out[...] = found[k * each : (k + 1) * each].astype(BF16)
    else:
        product[...] = found
        for k, out in enumerate(outs):
            start = pl.multiple_of(lax.rem(row + k, n_row) * each, each)
            out[...] = product[pl.ds(start, each), :].astype(BF16)


def exchange(chunks, axis):
    n = len(chunks)
    return [
        chunk if k == 0 else lax.ppermute(chunk, axis, [(i, (i + k) % n) for i in range(n)])
        for k, chunk in enumerate(chunks)
    ]


def total_of(parts):
    return sum(part.astype(F32) for part in parts).astype(BF16)


def call(kernel, shapes, scratch, *args, after=()):
    given = len(args)

    def body(*refs):
        kernel(*refs[:given], *refs[given + len(after) :])

    return pl.pallas_call(
        body,
        out_shape=[jax.ShapeDtypeStruct(shape, BF16) for shape in shapes],
        in_specs=[VMEM] * len(args) + [ANY] * len(after),
        out_specs=[VMEM] * len(shapes),
        scratch_shapes=scratch,
        compiler_params=pltpu.CompilerParams(**PARAMS),
    )(*args, *after)


def local(layers, table, fitting, owner, local_slice, block_index, weight_index):
    n_layer, n_row = lax.axis_size("layer"), lax.axis_size("row")
    rows_dev, columns = layers.shape[1:]
    entries = owner.shape[1]
    weights, slice_rows, block_rows = table.shape
    points, actuators = fitting.shape
    owned = points // slice_rows
    chunk = columns // n_row
    halves = 2 if chunk % 32 == 0 else 1
    per_half = columns // halves
    each = per_half // n_layer

    indices = jnp.concatenate([owner[:, :, 0], local_slice, block_index, weight_index], 0)
    parts, before = [], ()
    for h in range(halves):
        turned = call(
            functools.partial(turn_kernel, n_layer, n_row, halves, h),
            [(each, rows_dev + (LANES if h == 0 else 0))] * n_layer,
            [pltpu.VMEM((CODE_ROWS, LANES), jnp.int32)],
            layers[0],
            indices,
            after=before,
        )
        before = (turned[0],)
        parts.append(exchange(turned, "layer"))
    (padded,) = call(
        pad_kernel,
        [(LANES // block_rows * weights, LANES, slice_rows)],
        [],
        jnp.swapaxes(table, 1, 2),
        after=before,
    )

    received, before = [], ()
    for h in range(halves):
        shares = call(
            functools.partial(pupil_kernel, n_layer, n_row, entries, entries),
            [(each, points)] * n_row,
            [
                pltpu.VMEM((n_row * owned, each, slice_rows), F32),
                pltpu.VMEM((n_layer * CODE_ROWS, LANES), jnp.int32),
                pltpu.SMEM((n_layer * CODE_ROWS, LANES), jnp.int32),
                pltpu.SemaphoreType.DMA,
            ],
            padded,
            *parts[0],
            *parts[h],
            after=before,
        )
        before = (shares[0],)
        received.append(exchange(shares, "row"))
    results = []
    for h in range(halves):
        (pupil,) = call(sum_kernel, [(each, points)], [], *received[h], after=before)
        pieces = exchange([pupil] * n_layer, "layer")
        partial = call(
            functools.partial(fit_kernel, n_layer, n_row),
            [(chunk // halves, actuators)] * n_row,
            [pltpu.VMEM((n_layer, each, points), BF16), pltpu.VMEM((per_half, actuators), F32)],
            fitting.T,
            *pieces,
        )
        before = (partial[0],)
        results.append(exchange(partial, "row"))
    return jnp.concatenate([total_of(result) for result in results], 0)


def solution(mesh):
    return jax.shard_map(
        local,
        mesh=mesh,
        in_specs=(
            P("layer", "row", "panel"),
            P(),
            P("row", "layer"),
            P("layer", "row", None),
            P("layer", "row"),
            P("layer", "row"),
            P("layer", "row"),
        ),
        out_specs=P(("panel", "row"), "layer"),
        check_vma=False,
    )
```

```python
import functools

import jax
import jax.numpy as jnp
from jax import lax
from jax.experimental import pallas as pl
from jax.experimental.pallas import tpu as pltpu
from jax.sharding import PartitionSpec as P

LANES = 128
CODE_ROWS = 16
F32, BF16 = jnp.float32, jnp.bfloat16
VMEM = pl.BlockSpec(memory_space=pltpu.VMEM)
ANY = pl.BlockSpec(memory_space=pl.ANY)
PARAMS = dict(vmem_limit_bytes=16 * 1024 * 1024)


def turn_kernel(n_layer, n_row, halves, half, layers_ref, extra_ref, *refs):
    outs, codes = refs[:n_layer], refs[-1]
    rows_dev, columns = layers_ref.shape
    per_half = columns // halves
    each = per_half // n_layer
    chunk, part = columns // n_row, columns // n_row // halves
    first = lax.axis_index("layer") * each
    row = lax.broadcasted_iota(jnp.int32, (per_half, columns), 0)
    col = lax.broadcasted_iota(jnp.int32, (per_half, columns), 1)
    place = lax.rem(row + first, per_half)
    wanted = (place // part) * chunk + lax.rem(place, part) + half * part
    pick = (col == wanted).astype(BF16)
    turned = lax.dot_general(
        pick, layers_ref[...], (((1,), (1,)), ((), ())), preferred_element_type=F32
    ).astype(BF16)
    for k, out in enumerate(outs):
        out[:, :rows_dev] = turned[k * each : (k + 1) * each]
    if half == 0:
        codes[...] = jnp.zeros_like(codes)
        codes[: extra_ref.shape[0], : extra_ref.shape[1]] = extra_ref[...]
        tail = codes[...].astype(F32).astype(BF16)
        for out in outs:
            out[:, rows_dev:] = jnp.zeros((each, LANES), BF16)
            out[:CODE_ROWS, rows_dev:] = tail


def pad_kernel(table_ref, padded):
    weights, block_rows = table_ref.shape[:2]
    padded[...] = jnp.zeros_like(padded)
    for half in range(LANES // block_rows):
        start = half * block_rows
        padded[half * weights : (half + 1) * weights, start : start + block_rows] = table_ref[...]


def pupil_kernel(n_layer, n_row, entries, unroll, padded, *refs):
    coded, parts = refs[:n_layer], refs[n_layer : 2 * n_layer]
    out, total, codes, code, sem = refs[-5:]
    weights = padded.shape[0] // 2
    owned = out.shape[2] // LANES
    for j, ref in enumerate(coded):
        tail = ref[:CODE_ROWS, ref.shape[1] - LANES :]
        codes[j * CODE_ROWS : (j + 1) * CODE_ROWS] = tail.astype(F32).astype(jnp.int32)
    copy = pltpu.make_async_copy(codes, code, sem)
    copy.start()
    total[...] = jnp.zeros_like(total)
    copy.wait()
    for j, part in enumerate(parts):
        base = j * CODE_ROWS

        def step(group, carry):
            terms = []
            for u in range(unroll):
                e = group * unroll + u
                block = code[base + 2, e]
                source = part[:, pl.ds(pl.multiple_of((block // 2) * LANES, LANES), LANES)]
                weight = padded[lax.rem(block, 2) * weights + code[base + 3, e]]
                dest = code[base, e] * owned + code[base + 1, e]
                terms.append((dest, jnp.dot(source, weight, preferred_element_type=F32)))
            for dest, term in terms:
                total[dest] += term
            return carry

        lax.fori_loop(0, entries // unroll, step, 0)
    for r in range(n_row):
        for s in range(owned):
            out[r, :, s * LANES : (s + 1) * LANES] = total[r * owned + s].astype(BF16)


def sum_kernel(parts_ref, out_ref):
    parts = [parts_ref[r].astype(F32) for r in range(parts_ref.shape[0])]
    out_ref[...] = sum(parts).astype(BF16)


def fit_kernel(n_layer, fitting_ref, *refs):
    pieces, (out, left) = refs[:n_layer], refs[n_layer:]
    me = lax.axis_index("layer")
    for j, piece in enumerate(pieces):
        left[lax.rem(me + n_layer - j, n_layer)] = piece[...]
    n_row, each, _ = out.shape
    found = lax.dot_general(
        left[...].reshape(n_row * each, left.shape[2]),
        fitting_ref[...],
        (((1,), (1,)), ((), ())),
        preferred_element_type=F32,
    )
    for r in range(n_row):
        out[r] = found[r * each : (r + 1) * each].astype(BF16)


def exchange(chunks, axis):
    n = len(chunks)
    return [
        chunk if k == 0 else lax.ppermute(chunk, axis, [(i, (i + k) % n) for i in range(n)])
        for k, chunk in enumerate(chunks)
    ]


def swap(chunks, axis):
    return lax.all_to_all(chunks, axis, split_axis=0, concat_axis=0, tiled=True)


def call(kernel, shapes, scratch, *args, after=()):
    given = len(args)

    def body(*refs):
        kernel(*refs[:given], *refs[given + len(after) :])

    return pl.pallas_call(
        body,
        out_shape=[jax.ShapeDtypeStruct(shape, BF16) for shape in shapes],
        in_specs=[VMEM] * len(args) + [ANY] * len(after),
        out_specs=[VMEM] * len(shapes),
        scratch_shapes=scratch,
        compiler_params=pltpu.CompilerParams(**PARAMS),
    )(*args, *after)


def local(layers, table, fitting, owner, local_slice, block_index, weight_index):
    n_layer, n_row = lax.axis_size("layer"), lax.axis_size("row")
    rows_dev, columns = layers.shape[1:]
    entries = owner.shape[1]
    weights, slice_rows, block_rows = table.shape
    points, actuators = fitting.shape
    owned = points // slice_rows
    chunk = columns // n_row
    halves = 2 if chunk % 32 == 0 else 1
    per_half = columns // halves
    each = per_half // n_layer

    indices = jnp.concatenate([owner[:, :, 0], local_slice, block_index, weight_index], 0)
    parts, before = [], ()
    for h in range(halves):
        turned = call(
            functools.partial(turn_kernel, n_layer, n_row, halves, h),
            [(each, rows_dev + (LANES if h == 0 else 0))] * n_layer,
            [pltpu.VMEM((CODE_ROWS, LANES), jnp.int32)],
            layers[0],
            indices,
            after=before,
        )
        before = (turned[0],)
        parts.append(exchange(turned, "layer"))
    (padded,) = call(
        pad_kernel,
        [(LANES // block_rows * weights, LANES, slice_rows)],
        [],
        jnp.swapaxes(table, 1, 2),
        after=before,
    )

    received, before = [], ()
    for h in range(halves):
        shares = call(
            functools.partial(pupil_kernel, n_layer, n_row, entries, entries),
            [(n_row, each, points)],
            [
                pltpu.VMEM((n_row * owned, each, slice_rows), F32),
                pltpu.VMEM((n_layer * CODE_ROWS, LANES), jnp.int32),
                pltpu.SMEM((n_layer * CODE_ROWS, LANES), jnp.int32),
                pltpu.SemaphoreType.DMA,
            ],
            padded,
            *parts[0],
            *parts[h],
            after=before,
        )
        before = (shares[0],)
        received.append(swap(shares[0], "row"))
    results = []
    for h in range(halves):
        (pupil,) = call(sum_kernel, [(each, points)], [], received[h], after=before)
        pieces = exchange([pupil] * n_layer, "layer")
        partial = call(
            functools.partial(fit_kernel, n_layer),
            [(n_row, chunk // halves, actuators)],
            [pltpu.VMEM((n_layer, each, points), BF16)],
            fitting.T,
            *pieces,
        )
        before = (partial[0],)
        results.append(swap(partial[0], "row"))
    sums = [result.astype(F32).sum(0).astype(BF16) for result in results]
    return jnp.concatenate(sums, 0)


def solution(mesh):
    return jax.shard_map(
        local,
        mesh=mesh,
        in_specs=(
            P("layer", "row", "panel"),
            P(),
            P("row", "layer"),
            P("layer", "row", None),
            P("layer", "row"),
            P("layer", "row"),
            P("layer", "row"),
        ),
        out_specs=P(("panel", "row"), "layer"),
        check_vma=False,
    )
```

```python
import functools

import jax
import jax.numpy as jnp
from jax import lax
from jax.experimental import pallas as pl
from jax.experimental.pallas import tpu as pltpu
from jax.sharding import PartitionSpec as P

LANES = 128
CODE_ROWS = 16
F32, BF16 = jnp.float32, jnp.bfloat16
VMEM = pl.BlockSpec(memory_space=pltpu.VMEM)
ANY = pl.BlockSpec(memory_space=pl.ANY)
PARAMS = dict(vmem_limit_bytes=16 * 1024 * 1024)


def turn_kernel(n_layer, n_row, halves, half, layers_ref, extra_ref, *refs):
    outs, codes = refs[:n_layer], refs[-1]
    rows_dev, columns = layers_ref.shape
    per_half = columns // halves
    each = per_half // n_layer
    chunk, part = columns // n_row, columns // n_row // halves
    me = lax.axis_index("layer")
    row = lax.broadcasted_iota(jnp.int32, (per_half, columns), 0)
    col = lax.broadcasted_iota(jnp.int32, (per_half, columns), 1)
    place = lax.bitwise_xor(row // each, me) * each + lax.rem(row, each)
    wanted = (place // part) * chunk + lax.rem(place, part) + half * part
    pick = (col == wanted).astype(BF16)
    turned = lax.dot_general(
        pick, layers_ref[...], (((1,), (1,)), ((), ())), preferred_element_type=F32
    ).astype(BF16)
    for k, out in enumerate(outs):
        out[:, :rows_dev] = turned[k * each : (k + 1) * each]
    if half == 0:
        codes[...] = jnp.zeros_like(codes)
        codes[: extra_ref.shape[0], : extra_ref.shape[1]] = extra_ref[...]
        tail = codes[...].astype(F32).astype(BF16)
        for out in outs:
            out[:, rows_dev:] = jnp.zeros((each, LANES), BF16)
            out[:CODE_ROWS, rows_dev:] = tail


def pad_kernel(table_ref, padded):
    weights, block_rows = table_ref.shape[:2]
    padded[...] = jnp.zeros_like(padded)
    for half in range(LANES // block_rows):
        start = half * block_rows
        padded[half * weights : (half + 1) * weights, start : start + block_rows] = table_ref[...]


def pupil_kernel(n_layer, n_row, entries, unroll, padded, *refs):
    coded, parts = refs[:n_layer], refs[n_layer : 2 * n_layer]
    keep, send, total, codes, code, sem = refs[-6:]
    weights = padded.shape[0] // 2
    owned = keep.shape[2] // LANES
    for j, ref in enumerate(coded):
        tail = ref[:CODE_ROWS, ref.shape[1] - LANES :]
        codes[j * CODE_ROWS : (j + 1) * CODE_ROWS] = tail.astype(F32).astype(jnp.int32)
    copy = pltpu.make_async_copy(codes, code, sem)
    copy.start()
    total[...] = jnp.zeros_like(total)
    copy.wait()
    for j, part in enumerate(parts):
        base = j * CODE_ROWS

        def step(group, carry):
            terms = []
            for u in range(unroll):
                e = group * unroll + u
                block = code[base + 2, e]
                source = part[:, pl.ds(pl.multiple_of((block // 2) * LANES, LANES), LANES)]
                weight = padded[lax.rem(block, 2) * weights + code[base + 3, e]]
                dest = code[base, e] * owned + code[base + 1, e]
                terms.append((dest, jnp.dot(source, weight, preferred_element_type=F32)))
            for dest, term in terms:
                total[dest] += term
            return carry

        lax.fori_loop(0, entries // unroll, step, 0)
    me = lax.axis_index("row")
    for k in range(n_row):
        base = lax.bitwise_xor(me, k) * owned
        out = send if k % 2 else keep
        for s in range(owned):
            out[k // 2, :, s * LANES : (s + 1) * LANES] = total[base + s].astype(out.dtype)


def sum_kernel(kept_ref, got_ref, out_ref):
    out_ref[...] = (kept_ref[0] + got_ref[0].astype(F32)).astype(BF16)


def fit_kernel(n_layer, n_row, fitting_ref, *refs):
    pieces, (keep, send, left, product) = refs[:n_layer], refs[n_layer:]
    me, row = lax.axis_index("layer"), lax.axis_index("row")
    aligned = n_layer == n_row
    for j, piece in enumerate(pieces):
        place = lax.bitwise_xor(me, j)
        left[lax.bitwise_xor(place, row) if aligned else place] = piece[...]
    columns = left.shape[0] * left.shape[1]
    found = lax.dot_general(
        left[...].reshape(columns, left.shape[2]),
        fitting_ref[...],
        (((1,), (1,)), ((), ())),
        preferred_element_type=F32,
    )
    each = columns // n_row
    if not aligned:
        product[...] = found
    for k in range(n_row):
        out = send if k % 2 else keep
        if aligned:
            part = found[k * each : (k + 1) * each]
        else:
            start = pl.multiple_of(lax.bitwise_xor(row, k) * each, each)
            part = product[pl.ds(start, each), :]
        out[k // 2] = part.astype(out.dtype)


def trade(chunk, axis, k):
    return lax.ppermute(chunk, axis, [(i, i ^ k) for i in range(lax.axis_size(axis))])


def exchange(chunks, axis):
    return [chunk if k == 0 else trade(chunk, axis, k) for k, chunk in enumerate(chunks)]


def gather(piece, axis):
    got = []
    for k in range(0, lax.axis_size(axis), 2):
        got.append(trade(piece, axis, k) if k else piece)
        got.append(trade(got[-1], axis, 1))
    return got


def reduce(keep, send, axis):
    step = 1
    while True:
        got = trade(send, axis, step)
        if keep.shape[0] == 1:
            return keep, got
        added = keep + got.astype(F32)
        keep, send = added[::2], added[1::2].astype(BF16)
        step *= 2


def call(kernel, shapes, scratch, *args, types=None, after=()):
    given = len(args)

    def body(*refs):
        kernel(*refs[:given], *refs[given + len(after) :])

    return pl.pallas_call(
        body,
        out_shape=[
            jax.ShapeDtypeStruct(shape, kind)
            for shape, kind in zip(shapes, types or [BF16] * len(shapes))
        ],
        in_specs=[VMEM] * len(args) + [ANY] * len(after),
        out_specs=[VMEM] * len(shapes),
        scratch_shapes=scratch,
        compiler_params=pltpu.CompilerParams(**PARAMS),
    )(*args, *after)


def local(layers, table, fitting, owner, local_slice, block_index, weight_index):
    n_layer, n_row = lax.axis_size("layer"), lax.axis_size("row")
    rows_dev, columns = layers.shape[1:]
    entries = owner.shape[1]
    weights, slice_rows, block_rows = table.shape
    points, actuators = fitting.shape
    owned = points // slice_rows
    chunk = columns // n_row
    halves = 2 if chunk % 32 == 0 else 1
    per_half = columns // halves
    each = per_half // n_layer

    indices = jnp.concatenate([owner[:, :, 0], local_slice, block_index, weight_index], 0)
    parts, before = [], ()
    for h in range(halves):
        turned = call(
            functools.partial(turn_kernel, n_layer, n_row, halves, h),
            [(each, rows_dev + (LANES if h == 0 else 0))] * n_layer,
            [pltpu.VMEM((CODE_ROWS, LANES), jnp.int32)],
            layers[0],
            indices,
            after=before,
        )
        before = (turned[0],)
        parts.append(exchange(turned, "layer"))
    (padded,) = call(
        pad_kernel,
        [(LANES // block_rows * weights, LANES, slice_rows)],
        [],
        jnp.swapaxes(table, 1, 2),
        after=before,
    )

    received, before = [], tuple(parts[-1][1:2])
    for h in range(halves):
        shares = call(
            functools.partial(pupil_kernel, n_layer, n_row, entries, entries),
            [(n_row // 2, each, points)] * 2,
            [
                pltpu.VMEM((n_row * owned, each, slice_rows), F32),
                pltpu.VMEM((n_layer * CODE_ROWS, LANES), jnp.int32),
                pltpu.SMEM((n_layer * CODE_ROWS, LANES), jnp.int32),
                pltpu.SemaphoreType.DMA,
            ],
            padded,
            *parts[0],
            *parts[h],
            types=(F32, BF16),
            after=before,
        )
        before = (shares[0],)
        received.append(shares)
    results = []
    for h in range(halves):
        kept, got = reduce(*received[h], "row")
        (pupil,) = call(sum_kernel, [(each, points)], [], kept, got, after=before)
        pieces = gather(pupil, "layer")
        partial = call(
            functools.partial(fit_kernel, n_layer, n_row),
            [(n_row // 2, chunk // halves, actuators)] * 2,
            [pltpu.VMEM((n_layer, each, points), BF16), pltpu.VMEM((per_half, actuators), F32)],
            fitting.T,
            *pieces,
            types=(F32, BF16),
        )
        before = (partial[0],)
        kept, got = reduce(*partial, "row")
        results.append((kept[0] + got[0].astype(F32)).astype(BF16))
    return jnp.concatenate(results, 0)


def solution(mesh):
    return jax.shard_map(
        local,
        mesh=mesh,
        in_specs=(
            P("layer", "row", "panel"),
            P(),
            P("row", "layer"),
            P("layer", "row", None),
            P("layer", "row"),
            P("layer", "row"),
            P("layer", "row"),
        ),
        out_specs=P(("panel", "row"), "layer"),
        check_vma=False,
    )
```

```python
import functools

import jax
import jax.numpy as jnp
from jax import lax
from jax.experimental import pallas as pl
from jax.experimental.pallas import tpu as pltpu
from jax.sharding import PartitionSpec as P

LANES = 128
CODE_ROWS = 16
F32, BF16 = jnp.float32, jnp.bfloat16
VMEM = pl.BlockSpec(memory_space=pltpu.VMEM)
ANY = pl.BlockSpec(memory_space=pl.ANY)
PARAMS = dict(vmem_limit_bytes=16 * 1024 * 1024)


def turn_kernel(n_layer, n_row, halves, half, layers_ref, extra_ref, *refs):
    outs, codes = refs[:n_layer], refs[-1]
    rows_dev, columns = layers_ref.shape
    per_half = columns // halves
    each = per_half // n_layer
    chunk, part = columns // n_row, columns // n_row // halves
    me = lax.axis_index("layer")
    row = lax.broadcasted_iota(jnp.int32, (per_half, columns), 0)
    col = lax.broadcasted_iota(jnp.int32, (per_half, columns), 1)
    place = lax.bitwise_xor(row // each, me) * each + lax.rem(row, each)
    wanted = (place // part) * chunk + lax.rem(place, part) + half * part
    pick = (col == wanted).astype(BF16)
    turned = lax.dot_general(
        pick, layers_ref[...], (((1,), (1,)), ((), ())), preferred_element_type=F32
    ).astype(BF16)
    for k, out in enumerate(outs):
        out[:, :rows_dev] = turned[k * each : (k + 1) * each]
    if half == 0:
        codes[...] = jnp.zeros_like(codes)
        codes[: extra_ref.shape[0], : extra_ref.shape[1]] = extra_ref[...]
        tail = codes[...].astype(F32).astype(BF16)
        for out in outs:
            out[:, rows_dev:] = jnp.zeros((each, LANES), BF16)
            out[:CODE_ROWS, rows_dev:] = tail


def pad_kernel(table_ref, padded):
    weights, block_rows = table_ref.shape[:2]
    padded[...] = jnp.zeros_like(padded)
    for half in range(LANES // block_rows):
        start = half * block_rows
        padded[half * weights : (half + 1) * weights, start : start + block_rows] = table_ref[...]


def pupil_kernel(n_layer, n_row, entries, unroll, padded, *refs):
    coded, parts = refs[:n_layer], refs[n_layer : 2 * n_layer]
    outs = refs[2 * n_layer : 2 * n_layer + n_row]
    total, codes, code, sem = refs[-4:]
    weights = padded.shape[0] // 2
    owned = outs[0].shape[1] // LANES
    for j, ref in enumerate(coded):
        tail = ref[:CODE_ROWS, ref.shape[1] - LANES :]
        codes[j * CODE_ROWS : (j + 1) * CODE_ROWS] = tail.astype(F32).astype(jnp.int32)
    copy = pltpu.make_async_copy(codes, code, sem)
    copy.start()
    total[...] = jnp.zeros_like(total)
    copy.wait()
    for j, part in enumerate(parts):
        base = j * CODE_ROWS

        def step(group, carry):
            terms = []
            for u in range(unroll):
                e = group * unroll + u
                block = code[base + 2, e]
                source = part[:, pl.ds(pl.multiple_of((block // 2) * LANES, LANES), LANES)]
                weight = padded[lax.rem(block, 2) * weights + code[base + 3, e]]
                dest = code[base, e] * owned + code[base + 1, e]
                terms.append((dest, jnp.dot(source, weight, preferred_element_type=F32)))
            for dest, term in terms:
                total[dest] += term
            return carry

        lax.fori_loop(0, entries // unroll, step, 0)
    me = lax.axis_index("row")
    for k, out in enumerate(outs):
        base = lax.bitwise_xor(me, k) * owned
        for s in range(owned):
            out[:, s * LANES : (s + 1) * LANES] = total[base + s].astype(BF16)


def sum_kernel(*refs):
    refs[-1][...] = sum(ref[...].astype(F32) for ref in refs[:-1]).astype(BF16)


def fit_kernel(n_layer, n_row, fitting_ref, *refs):
    pieces, outs = refs[:n_layer], refs[n_layer : n_layer + n_row]
    left, product = refs[-2], refs[-1]
    aligned = n_layer == n_row
    me, row = lax.axis_index("layer"), lax.axis_index("row")
    for j, piece in enumerate(pieces):
        place = lax.bitwise_xor(me, j)
        left[lax.bitwise_xor(place, row) if aligned else place] = piece[...]
    columns = left.shape[0] * left.shape[1]
    found = lax.dot_general(
        left[...].reshape(columns, left.shape[2]),
        fitting_ref[...],
        (((1,), (1,)), ((), ())),
        preferred_element_type=F32,
    )
    each = columns // n_row
    if aligned:
        for k, out in enumerate(outs):
            out[...] = found[k * each : (k + 1) * each].astype(BF16)
    else:
        product[...] = found
        for k, out in enumerate(outs):
            start = pl.multiple_of(lax.bitwise_xor(row, k) * each, each)
            out[...] = product[pl.ds(start, each), :].astype(BF16)


def exchange(chunks, axis):
    n = len(chunks)
    return [
        chunk if k == 0 else lax.ppermute(chunk, axis, [(i, i ^ k) for i in range(n)])
        for k, chunk in enumerate(chunks)
    ]


def total_of(parts):
    return sum(part.astype(F32) for part in parts).astype(BF16)


def call(kernel, shapes, scratch, *args, after=()):
    given = len(args)

    def body(*refs):
        kernel(*refs[:given], *refs[given + len(after) :])

    return pl.pallas_call(
        body,
        out_shape=[jax.ShapeDtypeStruct(shape, BF16) for shape in shapes],
        in_specs=[VMEM] * len(args) + [ANY] * len(after),
        out_specs=[VMEM] * len(shapes),
        scratch_shapes=scratch,
        compiler_params=pltpu.CompilerParams(**PARAMS),
    )(*args, *after)


def local(layers, table, fitting, owner, local_slice, block_index, weight_index):
    n_layer, n_row = lax.axis_size("layer"), lax.axis_size("row")
    rows_dev, columns = layers.shape[1:]
    entries = owner.shape[1]
    weights, slice_rows, block_rows = table.shape
    points, actuators = fitting.shape
    owned = points // slice_rows
    chunk = columns // n_row
    halves = 2 if chunk % 32 == 0 else 1
    per_half = columns // halves
    each = per_half // n_layer

    indices = jnp.concatenate([owner[:, :, 0], local_slice, block_index, weight_index], 0)
    parts, before = [], ()
    for h in range(halves):
        turned = call(
            functools.partial(turn_kernel, n_layer, n_row, halves, h),
            [(each, rows_dev + (LANES if h == 0 else 0))] * n_layer,
            [pltpu.VMEM((CODE_ROWS, LANES), jnp.int32)],
            layers[0],
            indices,
            after=before,
        )
        before = (turned[0],)
        parts.append(exchange(turned, "layer"))
    (padded,) = call(
        pad_kernel,
        [(LANES // block_rows * weights, LANES, slice_rows)],
        [],
        jnp.swapaxes(table, 1, 2),
        after=before,
    )

    received, before = [], ()
    for h in range(halves):
        shares = call(
            functools.partial(pupil_kernel, n_layer, n_row, entries, entries),
            [(each, points)] * n_row,
            [
                pltpu.VMEM((n_row * owned, each, slice_rows), F32),
                pltpu.VMEM((n_layer * CODE_ROWS, LANES), jnp.int32),
                pltpu.SMEM((n_layer * CODE_ROWS, LANES), jnp.int32),
                pltpu.SemaphoreType.DMA,
            ],
            padded,
            *parts[0],
            *parts[h],
            after=before,
        )
        before = (shares[0],)
        received.append(exchange(shares, "row"))
    pupils = []
    for h in range(halves):
        pupils += call(sum_kernel, [(each, points)], [], *received[h], after=before)
    results = []
    for h in range(halves):
        pieces = exchange([pupils[h]] * n_layer, "layer")
        partial = call(
            functools.partial(fit_kernel, n_layer, n_row),
            [(chunk // halves, actuators)] * n_row,
            [pltpu.VMEM((n_layer, each, points), BF16), pltpu.VMEM((per_half, actuators), F32)],
            fitting.T,
            *pieces,
            after=pupils[h + 1 :],
        )
        results.append(exchange(partial, "row"))
    return jnp.concatenate([total_of(result) for result in results], 0)


def solution(mesh):
    return jax.shard_map(
        local,
        mesh=mesh,
        in_specs=(
            P("layer", "row", "panel"),
            P(),
            P("row", "layer"),
            P("layer", "row", None),
            P("layer", "row"),
            P("layer", "row"),
            P("layer", "row"),
        ),
        out_specs=P(("panel", "row"), "layer"),
        check_vma=False,
    )
```

```python
import functools

import jax
import jax.numpy as jnp
from jax import lax
from jax.experimental import pallas as pl
from jax.experimental.pallas import tpu as pltpu
from jax.sharding import PartitionSpec as P

LANES = 128
CODE_ROWS = 16
F32, BF16 = jnp.float32, jnp.bfloat16
VMEM = pl.BlockSpec(memory_space=pltpu.VMEM)
ANY = pl.BlockSpec(memory_space=pl.ANY)
PARAMS = dict(vmem_limit_bytes=16 * 1024 * 1024)


def turn_kernel(n_layer, n_row, halves, half, layers_ref, extra_ref, *refs):
    outs, codes = refs[:n_layer], refs[-1]
    rows_dev, columns = layers_ref.shape
    per_half = columns // halves
    each = per_half // n_layer
    chunk, part = columns // n_row, columns // n_row // halves
    me = lax.axis_index("layer")
    row = lax.broadcasted_iota(jnp.int32, (per_half, columns), 0)
    col = lax.broadcasted_iota(jnp.int32, (per_half, columns), 1)
    place = lax.bitwise_xor(row // each, me) * each + lax.rem(row, each)
    wanted = (place // part) * chunk + lax.rem(place, part) + half * part
    pick = (col == wanted).astype(BF16)
    turned = lax.dot_general(
        pick, layers_ref[...], (((1,), (1,)), ((), ())), preferred_element_type=F32
    ).astype(BF16)
    for i, out in enumerate(outs):
        k = (n_layer - i) % n_layer
        out[:, :rows_dev] = turned[k * each : (k + 1) * each]
    if half == 0:
        codes[...] = jnp.zeros_like(codes)
        codes[: extra_ref.shape[0], : extra_ref.shape[1]] = extra_ref[...]
        tail = codes[...].astype(F32).astype(BF16)
        for out in outs:
            out[:, rows_dev:] = jnp.zeros((each, LANES), BF16)
            out[:CODE_ROWS, rows_dev:] = tail


def pad_kernel(table_ref, padded):
    weights, block_rows = table_ref.shape[:2]
    padded[...] = jnp.zeros_like(padded)
    for half in range(LANES // block_rows):
        start = half * block_rows
        padded[half * weights : (half + 1) * weights, start : start + block_rows] = table_ref[...]


def pupil_kernel(n_layer, n_row, entries, unroll, padded, *refs):
    coded, parts = refs[:n_layer], refs[n_layer : 2 * n_layer]
    outs = refs[2 * n_layer : 2 * n_layer + n_row]
    total, codes, code, sem = refs[-4:]
    weights = padded.shape[0] // 2
    owned = outs[0].shape[1] // LANES
    for j, ref in enumerate(coded):
        tail = ref[:CODE_ROWS, ref.shape[1] - LANES :]
        codes[j * CODE_ROWS : (j + 1) * CODE_ROWS] = tail.astype(F32).astype(jnp.int32)
    copy = pltpu.make_async_copy(codes, code, sem)
    copy.start()
    total[...] = jnp.zeros_like(total)
    copy.wait()
    for j, part in enumerate(parts):
        base = j * CODE_ROWS

        def step(group, carry):
            terms = []
            for u in range(unroll):
                e = group * unroll + u
                block = code[base + 2, e]
                source = part[:, pl.ds(pl.multiple_of((block // 2) * LANES, LANES), LANES)]
                weight = padded[lax.rem(block, 2) * weights + code[base + 3, e]]
                dest = code[base, e] * owned + code[base + 1, e]
                terms.append((dest, jnp.dot(source, weight, preferred_element_type=F32)))
            for dest, term in terms:
                total[dest] += term
            return carry

        lax.fori_loop(0, entries // unroll, step, 0)
    me = lax.axis_index("row")
    for i, out in enumerate(outs):
        k = (n_row - i) % n_row
        base = lax.bitwise_xor(me, k) * owned
        for s in range(owned):
            out[:, s * LANES : (s + 1) * LANES] = total[base + s].astype(BF16)


def sum_kernel(*refs):
    refs[-1][...] = sum(ref[...].astype(F32) for ref in refs[:-1]).astype(BF16)


def fit_kernel(n_layer, n_row, fitting_ref, *refs):
    pieces, outs = refs[:n_layer], refs[n_layer : n_layer + n_row]
    left, product = refs[-2], refs[-1]
    aligned = n_layer == n_row
    me, row = lax.axis_index("layer"), lax.axis_index("row")
    for j, piece in enumerate(pieces):
        place = lax.bitwise_xor(me, j)
        left[lax.bitwise_xor(place, row) if aligned else place] = piece[...]
    columns = left.shape[0] * left.shape[1]
    found = lax.dot_general(
        left[...].reshape(columns, left.shape[2]),
        fitting_ref[...],
        (((1,), (1,)), ((), ())),
        preferred_element_type=F32,
    )
    each = columns // n_row
    if aligned:
        for i, out in enumerate(outs):
            k = (n_row - i) % n_row
            out[...] = found[k * each : (k + 1) * each].astype(BF16)
    else:
        product[...] = found
        for i, out in enumerate(outs):
            k = (n_row - i) % n_row
            start = pl.multiple_of(lax.bitwise_xor(row, k) * each, each)
            out[...] = product[pl.ds(start, each), :].astype(BF16)


def exchange(chunks, axis, sign=-1):
    n = len(chunks)
    return [
        lax.ppermute(chunk, axis, [(j, j ^ (sign * i % n)) for j in range(n)]) if i else chunk
        for i, chunk in enumerate(chunks)
    ]


def total_of(parts):
    return sum(part.astype(F32) for part in parts).astype(BF16)


def call(kernel, shapes, scratch, *args, after=()):
    given = len(args)

    def body(*refs):
        kernel(*refs[:given], *refs[given + len(after) :])

    return pl.pallas_call(
        body,
        out_shape=[jax.ShapeDtypeStruct(shape, BF16) for shape in shapes],
        in_specs=[VMEM] * len(args) + [ANY] * len(after),
        out_specs=[VMEM] * len(shapes),
        scratch_shapes=scratch,
        compiler_params=pltpu.CompilerParams(**PARAMS),
    )(*args, *after)


def local(layers, table, fitting, owner, local_slice, block_index, weight_index):
    n_layer, n_row = lax.axis_size("layer"), lax.axis_size("row")
    rows_dev, columns = layers.shape[1:]
    entries = owner.shape[1]
    weights, slice_rows, block_rows = table.shape
    points, actuators = fitting.shape
    owned = points // slice_rows
    chunk = columns // n_row
    halves = 2 if chunk % 32 == 0 else 1
    per_half = columns // halves
    each = per_half // n_layer

    indices = jnp.concatenate([owner[:, :, 0], local_slice, block_index, weight_index], 0)
    parts, before = [], ()
    for h in range(halves):
        turned = call(
            functools.partial(turn_kernel, n_layer, n_row, halves, h),
            [(each, rows_dev + (LANES if h == 0 else 0))] * n_layer,
            [pltpu.VMEM((CODE_ROWS, LANES), jnp.int32)],
            layers[0],
            indices,
            after=before,
        )
        before = (turned[0],)
        parts.append(exchange(turned, "layer"))
    (padded,) = call(
        pad_kernel,
        [(LANES // block_rows * weights, LANES, slice_rows)],
        [],
        jnp.swapaxes(table, 1, 2),
        after=before,
    )

    received, before = [], ()
    for h in range(halves):
        shares = call(
            functools.partial(pupil_kernel, n_layer, n_row, entries, entries),
            [(each, points)] * n_row,
            [
                pltpu.VMEM((n_row * owned, each, slice_rows), F32),
                pltpu.VMEM((n_layer * CODE_ROWS, LANES), jnp.int32),
                pltpu.SMEM((n_layer * CODE_ROWS, LANES), jnp.int32),
                pltpu.SemaphoreType.DMA,
            ],
            padded,
            *parts[0],
            *parts[h],
            after=before,
        )
        before = (shares[0],)
        received.append(exchange(shares, "row"))
    results = []
    for h in range(halves):
        (pupil,) = call(sum_kernel, [(each, points)], [], *received[h], after=before)
        pieces = exchange([pupil] * n_layer, "layer", 1)
        partial = call(
            functools.partial(fit_kernel, n_layer, n_row),
            [(chunk // halves, actuators)] * n_row,
            [pltpu.VMEM((n_layer, each, points), BF16), pltpu.VMEM((per_half, actuators), F32)],
            fitting.T,
            *pieces,
        )
        before = (partial[0],)
        results.append(exchange(partial, "row"))
    return jnp.concatenate([total_of(result) for result in results], 0)


def solution(mesh):
    return jax.shard_map(
        local,
        mesh=mesh,
        in_specs=(
            P("layer", "row", "panel"),
            P(),
            P("row", "layer"),
            P("layer", "row", None),
            P("layer", "row"),
            P("layer", "row"),
            P("layer", "row"),
        ),
        out_specs=P(("panel", "row"), "layer"),
        check_vma=False,
    )
```

```python
import functools

import jax
import jax.numpy as jnp
from jax import lax
from jax.experimental import pallas as pl
from jax.experimental.pallas import tpu as pltpu
from jax.sharding import PartitionSpec as P

LANES = 128
CODE_ROWS = 16
F32, BF16 = jnp.float32, jnp.bfloat16
VMEM = pl.BlockSpec(memory_space=pltpu.VMEM)
ANY = pl.BlockSpec(memory_space=pl.ANY)
PARAMS = dict(vmem_limit_bytes=16 * 1024 * 1024)


def turn_kernel(n_layer, n_row, halves, half, layers_ref, extra_ref, *refs):
    outs, codes = refs[:n_layer], refs[-1]
    rows_dev, columns = layers_ref.shape
    per_half = columns // halves
    each = per_half // n_layer
    chunk, part = columns // n_row, columns // n_row // halves
    me = lax.axis_index("layer")
    row = lax.broadcasted_iota(jnp.int32, (per_half, columns), 0)
    col = lax.broadcasted_iota(jnp.int32, (per_half, columns), 1)
    place = lax.bitwise_xor(row // each, me) * each + lax.rem(row, each)
    wanted = (place // part) * chunk + lax.rem(place, part) + half * part
    pick = (col == wanted).astype(BF16)
    turned = lax.dot_general(
        pick, layers_ref[...], (((1,), (1,)), ((), ())), preferred_element_type=F32
    ).astype(BF16)
    for i, out in enumerate(outs):
        k = (n_layer - i) % n_layer
        out[:, :rows_dev] = turned[k * each : (k + 1) * each]
    if half == 0:
        codes[...] = jnp.zeros_like(codes)
        codes[: extra_ref.shape[0], : extra_ref.shape[1]] = extra_ref[...]
        tail = codes[...].astype(F32).astype(BF16)
        for out in outs:
            out[:, rows_dev:] = jnp.zeros((each, LANES), BF16)
            out[:CODE_ROWS, rows_dev:] = tail


def pad_kernel(table_ref, padded):
    weights, block_rows = table_ref.shape[:2]
    padded[...] = jnp.zeros_like(padded)
    for half in range(LANES // block_rows):
        start = half * block_rows
        padded[half * weights : (half + 1) * weights, start : start + block_rows] = table_ref[...]


def pupil_kernel(n_layer, n_row, entries, unroll, padded, *refs):
    coded, parts = refs[:n_layer], refs[n_layer : 2 * n_layer]
    outs = refs[2 * n_layer : 2 * n_layer + n_row]
    total, codes, code, sem = refs[-4:]
    weights = padded.shape[0] // 2
    owned = outs[0].shape[1] // LANES
    for j, ref in enumerate(coded):
        tail = ref[:CODE_ROWS, ref.shape[1] - LANES :]
        codes[j * CODE_ROWS : (j + 1) * CODE_ROWS] = tail.astype(F32).astype(jnp.int32)
    copy = pltpu.make_async_copy(codes, code, sem)
    copy.start()
    total[...] = jnp.zeros_like(total)
    copy.wait()
    for j, part in enumerate(parts):
        base = j * CODE_ROWS

        def step(group, carry):
            terms = []
            for u in range(unroll):
                e = group * unroll + u
                block = code[base + 2, e]
                source = part[:, pl.ds(pl.multiple_of((block // 2) * LANES, LANES), LANES)]
                weight = padded[lax.rem(block, 2) * weights + code[base + 3, e]]
                dest = code[base, e] * owned + code[base + 1, e]
                terms.append((dest, jnp.dot(source, weight, preferred_element_type=F32)))
            for dest, term in terms:
                total[dest] += term
            return carry

        lax.fori_loop(0, entries // unroll, step, 0)
    me = lax.axis_index("row")
    for i, out in enumerate(outs):
        k = (n_row - i) % n_row
        base = lax.bitwise_xor(me, k) * owned
        for s in range(owned):
            out[:, s * LANES : (s + 1) * LANES] = total[base + s].astype(BF16)


def sum_kernel(*refs):
    refs[-1][...] = sum(ref[...].astype(F32) for ref in refs[:-1]).astype(BF16)


def fit_kernel(n_layer, n_row, fitting_ref, *refs):
    pieces, outs = refs[:n_layer], refs[n_layer : n_layer + n_row]
    left, product = refs[-2], refs[-1]
    aligned = n_layer == n_row
    me, row = lax.axis_index("layer"), lax.axis_index("row")
    for j, piece in enumerate(pieces):
        place = lax.bitwise_xor(me, j)
        left[lax.bitwise_xor(place, row) if aligned else place] = piece[...]
    columns = left.shape[0] * left.shape[1]
    found = lax.dot_general(
        left[...].reshape(columns, left.shape[2]),
        fitting_ref[...],
        (((1,), (1,)), ((), ())),
        preferred_element_type=F32,
    )
    each = columns // n_row
    if aligned:
        for i, out in enumerate(outs):
            k = (n_row - i) % n_row
            out[...] = found[k * each : (k + 1) * each].astype(BF16)
    else:
        product[...] = found
        for i, out in enumerate(outs):
            k = (n_row - i) % n_row
            start = pl.multiple_of(lax.bitwise_xor(row, k) * each, each)
            out[...] = product[pl.ds(start, each), :].astype(BF16)


def exchange(chunks, axis, sign=-1):
    n = len(chunks)
    return [
        lax.ppermute(chunk, axis, [(j, j ^ (sign * i % n)) for j in range(n)]) if i else chunk
        for i, chunk in enumerate(chunks)
    ]


def total_of(parts):
    return sum(part.astype(F32) for part in parts).astype(BF16)


def call(kernel, shapes, scratch, *args, after=()):
    given = len(args)

    def body(*refs):
        kernel(*refs[:given], *refs[given + len(after) :])

    return pl.pallas_call(
        body,
        out_shape=[jax.ShapeDtypeStruct(shape, BF16) for shape in shapes],
        in_specs=[VMEM] * len(args) + [ANY] * len(after),
        out_specs=[VMEM] * len(shapes),
        scratch_shapes=scratch,
        compiler_params=pltpu.CompilerParams(**PARAMS),
    )(*args, *after)


def local(layers, table, fitting, owner, local_slice, block_index, weight_index):
    n_layer, n_row = lax.axis_size("layer"), lax.axis_size("row")
    rows_dev, columns = layers.shape[1:]
    entries = owner.shape[1]
    weights, slice_rows, block_rows = table.shape
    points, actuators = fitting.shape
    owned = points // slice_rows
    chunk = columns // n_row
    halves = 2 if chunk % 32 == 0 else 1
    per_half = columns // halves
    each = per_half // n_layer

    indices = jnp.concatenate([owner[:, :, 0], local_slice, block_index, weight_index], 0)
    parts, before = [], ()
    for h in range(halves):
        turned = call(
            functools.partial(turn_kernel, n_layer, n_row, halves, h),
            [(each, rows_dev + (LANES if h == 0 else 0))] * n_layer,
            [pltpu.VMEM((CODE_ROWS, LANES), jnp.int32)],
            layers[0],
            indices,
            after=before,
        )
        before = (turned[0],)
        parts.append(exchange(turned, "layer"))
    (padded,) = call(
        pad_kernel,
        [(LANES // block_rows * weights, LANES, slice_rows)],
        [],
        jnp.swapaxes(table, 1, 2),
        after=before,
    )

    received, before = [], ()
    for h in range(halves):
        shares = call(
            functools.partial(pupil_kernel, n_layer, n_row, entries, entries),
            [(each, points)] * n_row,
            [
                pltpu.VMEM((n_row * owned, each, slice_rows), F32),
                pltpu.VMEM((n_layer * CODE_ROWS, LANES), jnp.int32),
                pltpu.SMEM((n_layer * CODE_ROWS, LANES), jnp.int32),
                pltpu.SemaphoreType.DMA,
            ],
            padded,
            *parts[0],
            *parts[h],
            after=before,
        )
        before = (shares[0],)
        received.append(exchange(shares, "row"))
    results, ahead = [], tuple(received[-1][1:2])
    for h in range(halves):
        (pupil,) = call(sum_kernel, [(each, points)], [], *received[h], after=before)
        pieces = exchange([pupil] * n_layer, "layer", 1)
        partial = call(
            functools.partial(fit_kernel, n_layer, n_row),
            [(chunk // halves, actuators)] * n_row,
            [pltpu.VMEM((n_layer, each, points), BF16), pltpu.VMEM((per_half, actuators), F32)],
            fitting.T,
            *pieces,
            after=ahead,
        )
        before = (partial[0],)
        results.append(exchange(partial, "row"))
        ahead = tuple(results[-1][1:2])
    return jnp.concatenate([total_of(result) for result in results], 0)


def solution(mesh):
    return jax.shard_map(
        local,
        mesh=mesh,
        in_specs=(
            P("layer", "row", "panel"),
            P(),
            P("row", "layer"),
            P("layer", "row", None),
            P("layer", "row"),
            P("layer", "row"),
            P("layer", "row"),
        ),
        out_specs=P(("panel", "row"), "layer"),
        check_vma=False,
    )
```

```python
import functools

import jax
import jax.numpy as jnp
from jax import lax
from jax.experimental import pallas as pl
from jax.experimental.pallas import tpu as pltpu
from jax.sharding import PartitionSpec as P

LANES = 128
CODE_ROWS = 16
F32, BF16 = jnp.float32, jnp.bfloat16
VMEM = pl.BlockSpec(memory_space=pltpu.VMEM)
ANY = pl.BlockSpec(memory_space=pl.ANY)
PARAMS = dict(vmem_limit_bytes=16 * 1024 * 1024)


def turn_kernel(n_layer, n_row, halves, half, layers_ref, extra_ref, *refs):
    outs, codes = refs[:n_layer], refs[-1]
    rows_dev, columns = layers_ref.shape
    per_half = columns // halves
    each = per_half // n_layer
    chunk, part = columns // n_row, columns // n_row // halves
    me = lax.axis_index("layer")
    row = lax.broadcasted_iota(jnp.int32, (per_half, columns), 0)
    col = lax.broadcasted_iota(jnp.int32, (per_half, columns), 1)
    place = lax.bitwise_xor(row // each, me) * each + lax.rem(row, each)
    wanted = (place // part) * chunk + lax.rem(place, part) + half * part
    pick = (col == wanted).astype(BF16)
    turned = lax.dot_general(
        pick, layers_ref[...], (((1,), (1,)), ((), ())), preferred_element_type=F32
    ).astype(BF16)
    for i, out in enumerate(outs):
        k = (n_layer - i) % n_layer
        out[:, :rows_dev] = turned[k * each : (k + 1) * each]
    if half == 0:
        codes[...] = jnp.zeros_like(codes)
        codes[: extra_ref.shape[0], : extra_ref.shape[1]] = extra_ref[...]
        tail = codes[...].astype(F32).astype(BF16)
        for out in outs:
            out[:, rows_dev:] = jnp.zeros((each, LANES), BF16)
            out[:CODE_ROWS, rows_dev:] = tail


def pad_kernel(table_ref, padded):
    weights, block_rows = table_ref.shape[:2]
    padded[...] = jnp.zeros_like(padded)
    for half in range(LANES // block_rows):
        start = half * block_rows
        padded[half * weights : (half + 1) * weights, start : start + block_rows] = table_ref[...]


def pupil_kernel(n_layer, n_row, entries, unroll, padded, *refs):
    coded, parts = refs[:n_layer], refs[n_layer : 2 * n_layer]
    outs = refs[2 * n_layer : 2 * n_layer + n_row]
    total, codes, code, sem = refs[-4:]
    weights = padded.shape[0] // 2
    owned = outs[0].shape[1] // LANES
    for j, ref in enumerate(coded):
        tail = ref[:CODE_ROWS, ref.shape[1] - LANES :]
        codes[j * CODE_ROWS : (j + 1) * CODE_ROWS] = tail.astype(F32).astype(jnp.int32)
    copy = pltpu.make_async_copy(codes, code, sem)
    copy.start()
    total[...] = jnp.zeros_like(total)
    copy.wait()
    for j, part in enumerate(parts):
        base = j * CODE_ROWS

        def step(group, carry):
            terms = []
            for u in range(unroll):
                e = group * unroll + u
                block = code[base + 2, e]
                source = part[:, pl.ds(pl.multiple_of((block // 2) * LANES, LANES), LANES)]
                weight = padded[lax.rem(block, 2) * weights + code[base + 3, e]]
                dest = code[base, e] * owned + code[base + 1, e]
                terms.append((dest, jnp.dot(source, weight, preferred_element_type=F32)))
            for dest, term in terms:
                total[dest] += term
            return carry

        lax.fori_loop(0, entries // unroll, step, 0)
    me = lax.axis_index("row")
    for i, out in enumerate(outs):
        k = (n_row - i) % n_row
        base = lax.bitwise_xor(me, k) * owned
        for s in range(owned):
            out[:, s * LANES : (s + 1) * LANES] = total[base + s].astype(BF16)


def sum_kernel(*refs):
    refs[-1][...] = sum(ref[...].astype(F32) for ref in refs[:-1]).astype(BF16)


def fit_kernel(n_layer, n_row, fitting_ref, *refs):
    pieces, outs = refs[:n_layer], refs[n_layer : n_layer + n_row]
    left, product = refs[-2], refs[-1]
    aligned = n_layer == n_row
    me, row = lax.axis_index("layer"), lax.axis_index("row")
    for j, piece in enumerate(pieces):
        place = lax.bitwise_xor(me, j)
        left[lax.bitwise_xor(place, row) if aligned else place] = piece[...]
    columns = left.shape[0] * left.shape[1]
    found = lax.dot_general(
        left[...].reshape(columns, left.shape[2]),
        fitting_ref[...],
        (((1,), (1,)), ((), ())),
        preferred_element_type=F32,
    )
    each = columns // n_row
    if aligned:
        for i, out in enumerate(outs):
            k = (n_row - i) % n_row
            out[...] = found[k * each : (k + 1) * each].astype(BF16)
    else:
        product[...] = found
        for i, out in enumerate(outs):
            k = (n_row - i) % n_row
            start = pl.multiple_of(lax.bitwise_xor(row, k) * each, each)
            out[...] = product[pl.ds(start, each), :].astype(BF16)


def trade(chunk, axis, k):
    return lax.ppermute(chunk, axis, [(j, j ^ k) for j in range(lax.axis_size(axis))])


def exchange(chunks, axis):
    n = len(chunks)
    return [trade(chunk, axis, n - i) if i else chunk for i, chunk in enumerate(chunks)]


def gather(piece, axis, paired):
    got = [piece]
    for k in range(1, lax.axis_size(axis)):
        got.append(trade(got[k - 1], axis, 1) if paired and k % 2 else trade(piece, axis, k))
    return got


def total_of(parts):
    return sum(part.astype(F32) for part in parts).astype(BF16)


def call(kernel, shapes, scratch, *args, after=()):
    given = len(args)

    def body(*refs):
        kernel(*refs[:given], *refs[given + len(after) :])

    return pl.pallas_call(
        body,
        out_shape=[jax.ShapeDtypeStruct(shape, BF16) for shape in shapes],
        in_specs=[VMEM] * len(args) + [ANY] * len(after),
        out_specs=[VMEM] * len(shapes),
        scratch_shapes=scratch,
        compiler_params=pltpu.CompilerParams(**PARAMS),
    )(*args, *after)


def local(layers, table, fitting, owner, local_slice, block_index, weight_index):
    n_layer, n_row = lax.axis_size("layer"), lax.axis_size("row")
    rows_dev, columns = layers.shape[1:]
    entries = owner.shape[1]
    weights, slice_rows, block_rows = table.shape
    points, actuators = fitting.shape
    owned = points // slice_rows
    chunk = columns // n_row
    halves = 2 if chunk % 32 == 0 else 1
    per_half = columns // halves
    each = per_half // n_layer

    indices = jnp.concatenate([owner[:, :, 0], local_slice, block_index, weight_index], 0)
    parts, before = [], ()
    for h in range(halves):
        turned = call(
            functools.partial(turn_kernel, n_layer, n_row, halves, h),
            [(each, rows_dev + (LANES if h == 0 else 0))] * n_layer,
            [pltpu.VMEM((CODE_ROWS, LANES), jnp.int32)],
            layers[0],
            indices,
            after=before,
        )
        before = (turned[0],)
        parts.append(exchange(turned, "layer"))
    (padded,) = call(
        pad_kernel,
        [(LANES // block_rows * weights, LANES, slice_rows)],
        [],
        jnp.swapaxes(table, 1, 2),
        after=before,
    )

    received, before = [], ()
    for h in range(halves):
        shares = call(
            functools.partial(pupil_kernel, n_layer, n_row, entries, entries),
            [(each, points)] * n_row,
            [
                pltpu.VMEM((n_row * owned, each, slice_rows), F32),
                pltpu.VMEM((n_layer * CODE_ROWS, LANES), jnp.int32),
                pltpu.SMEM((n_layer * CODE_ROWS, LANES), jnp.int32),
                pltpu.SemaphoreType.DMA,
            ],
            padded,
            *parts[0],
            *parts[h],
            after=before,
        )
        before = (shares[0],)
        if h > 0:
            shares, received[-1] = lax.optimization_barrier((shares, received[-1]))
        received.append(exchange(shares, "row"))
    results, ahead = [], tuple(received[-1][1:2])
    for h in range(halves):
        (pupil,) = call(sum_kernel, [(each, points)], [], *received[h], after=before)
        pieces = gather(pupil, "layer", h == 0)
        partial = call(
            functools.partial(fit_kernel, n_layer, n_row),
            [(chunk // halves, actuators)] * n_row,
            [pltpu.VMEM((n_layer, each, points), BF16), pltpu.VMEM((per_half, actuators), F32)],
            fitting.T,
            *pieces,
            after=ahead,
        )
        before = (partial[0],)
        results.append(exchange(partial, "row"))
        ahead = tuple(results[-1][1:2])
    return jnp.concatenate([total_of(result) for result in results], 0)


def solution(mesh):
    return jax.shard_map(
        local,
        mesh=mesh,
        in_specs=(
            P("layer", "row", "panel"),
            P(),
            P("row", "layer"),
            P("layer", "row", None),
            P("layer", "row"),
            P("layer", "row"),
            P("layer", "row"),
        ),
        out_specs=P(("panel", "row"), "layer"),
        check_vma=False,
    )
```

```python
import functools

import jax
import jax.numpy as jnp
from jax import lax
from jax.experimental import pallas as pl
from jax.experimental.pallas import tpu as pltpu
from jax.sharding import PartitionSpec as P

LANES = 128
CODE_ROWS = 16
F32, BF16 = jnp.float32, jnp.bfloat16
VMEM = pl.BlockSpec(memory_space=pltpu.VMEM)
ANY = pl.BlockSpec(memory_space=pl.ANY)
PARAMS = dict(vmem_limit_bytes=16 * 1024 * 1024)


def turn_kernel(n_layer, n_row, halves, half, layers_ref, extra_ref, *refs):
    outs, codes = refs[:n_layer], refs[-1]
    rows_dev, columns = layers_ref.shape
    per_half = columns // halves
    each = per_half // n_layer
    chunk, part = columns // n_row, columns // n_row // halves
    me = lax.axis_index("layer")
    row = lax.broadcasted_iota(jnp.int32, (per_half, columns), 0)
    col = lax.broadcasted_iota(jnp.int32, (per_half, columns), 1)
    place = lax.bitwise_xor(row // each, me) * each + lax.rem(row, each)
    wanted = (place // part) * chunk + lax.rem(place, part) + half * part
    pick = (col == wanted).astype(BF16)
    turned = lax.dot_general(
        pick, layers_ref[...], (((1,), (1,)), ((), ())), preferred_element_type=F32
    ).astype(BF16)
    for i, out in enumerate(outs):
        k = (n_layer - i) % n_layer
        out[:, :rows_dev] = turned[k * each : (k + 1) * each]
    if half == 0:
        codes[...] = jnp.zeros_like(codes)
        codes[: extra_ref.shape[0], : extra_ref.shape[1]] = extra_ref[...]
        tail = codes[...].astype(F32).astype(BF16)
        for out in outs:
            out[:, rows_dev:] = jnp.zeros((each, LANES), BF16)
            out[:CODE_ROWS, rows_dev:] = tail


def pad_kernel(table_ref, padded):
    weights, block_rows = table_ref.shape[:2]
    padded[...] = jnp.zeros_like(padded)
    for half in range(LANES // block_rows):
        start = half * block_rows
        padded[half * weights : (half + 1) * weights, start : start + block_rows] = table_ref[...]


def pupil_kernel(n_layer, n_row, entries, unroll, padded, *refs):
    coded, parts = refs[:n_layer], refs[n_layer : 2 * n_layer]
    outs = refs[2 * n_layer : 2 * n_layer + n_row]
    total, codes, code, sem = refs[-4:]
    weights = padded.shape[0] // 2
    owned = outs[0].shape[1] // LANES
    for j, ref in enumerate(coded):
        tail = ref[:CODE_ROWS, ref.shape[1] - LANES :]
        codes[j * CODE_ROWS : (j + 1) * CODE_ROWS] = tail.astype(F32).astype(jnp.int32)
    copy = pltpu.make_async_copy(codes, code, sem)
    copy.start()
    total[...] = jnp.zeros_like(total)
    copy.wait()
    for j, part in enumerate(parts):
        base = j * CODE_ROWS

        def step(group, carry):
            terms = []
            for u in range(unroll):
                e = group * unroll + u
                block = code[base + 2, e]
                source = part[:, pl.ds(pl.multiple_of((block // 2) * LANES, LANES), LANES)]
                weight = padded[lax.rem(block, 2) * weights + code[base + 3, e]]
                dest = code[base, e] * owned + code[base + 1, e]
                terms.append((dest, jnp.dot(source, weight, preferred_element_type=F32)))
            for dest, term in terms:
                total[dest] += term
            return carry

        lax.fori_loop(0, entries // unroll, step, 0)
    me = lax.axis_index("row")
    for i, out in enumerate(outs):
        k = (n_row - i) % n_row
        base = lax.bitwise_xor(me, k) * owned
        for s in range(owned):
            out[:, s * LANES : (s + 1) * LANES] = total[base + s].astype(BF16)


def sum_kernel(*refs):
    refs[-1][...] = sum(ref[...].astype(F32) for ref in refs[:-1]).astype(BF16)


def fit_kernel(n_layer, n_row, fitting_ref, *refs):
    pieces, outs = refs[:n_layer], refs[n_layer : n_layer + n_row]
    left, product = refs[-2], refs[-1]
    aligned = n_layer == n_row
    me, row = lax.axis_index("layer"), lax.axis_index("row")
    for j, piece in enumerate(pieces):
        place = lax.bitwise_xor(me, j)
        left[lax.bitwise_xor(place, row) if aligned else place] = piece[...]
    columns = left.shape[0] * left.shape[1]
    found = lax.dot_general(
        left[...].reshape(columns, left.shape[2]),
        fitting_ref[...],
        (((1,), (1,)), ((), ())),
        preferred_element_type=F32,
    )
    each = columns // n_row
    if aligned:
        for i, out in enumerate(outs):
            k = (n_row - i) % n_row
            out[...] = found[k * each : (k + 1) * each].astype(BF16)
    else:
        product[...] = found
        for i, out in enumerate(outs):
            k = (n_row - i) % n_row
            start = pl.multiple_of(lax.bitwise_xor(row, k) * each, each)
            out[...] = product[pl.ds(start, each), :].astype(BF16)


def trade(chunk, axis, k):
    return lax.ppermute(chunk, axis, [(j, j ^ k) for j in range(lax.axis_size(axis))])


def exchange(chunks, axis):
    n = len(chunks)
    return [trade(chunk, axis, n - i) if i else chunk for i, chunk in enumerate(chunks)]


def gather(piece, axis, paired):
    got = [piece]
    for k in range(1, lax.axis_size(axis)):
        got.append(trade(got[k - 1], axis, 1) if paired and k % 2 else trade(piece, axis, k))
    return got


def total_of(parts):
    return sum(part.astype(F32) for part in parts).astype(BF16)


def call(kernel, shapes, scratch, *args, after=()):
    given = len(args)

    def body(*refs):
        kernel(*refs[:given], *refs[given + len(after) :])

    return pl.pallas_call(
        body,
        out_shape=[jax.ShapeDtypeStruct(shape, BF16) for shape in shapes],
        in_specs=[VMEM] * len(args) + [ANY] * len(after),
        out_specs=[VMEM] * len(shapes),
        scratch_shapes=scratch,
        compiler_params=pltpu.CompilerParams(**PARAMS),
    )(*args, *after)


def local(layers, table, fitting, owner, local_slice, block_index, weight_index):
    n_layer, n_row = lax.axis_size("layer"), lax.axis_size("row")
    rows_dev, columns = layers.shape[1:]
    entries = owner.shape[1]
    weights, slice_rows, block_rows = table.shape
    points, actuators = fitting.shape
    owned = points // slice_rows
    chunk = columns // n_row
    halves = 2 if chunk % 32 == 0 else 1
    per_half = columns // halves
    each = per_half // n_layer

    indices = jnp.concatenate([owner[:, :, 0], local_slice, block_index, weight_index], 0)
    parts, before = [], ()
    for h in range(halves):
        turned = call(
            functools.partial(turn_kernel, n_layer, n_row, halves, h),
            [(each, rows_dev + (LANES if h == 0 else 0))] * n_layer,
            [pltpu.VMEM((CODE_ROWS, LANES), jnp.int32)],
            layers[0],
            indices,
            after=before,
        )
        before = (turned[0],)
        if h > 0:
            turned, parts[-1][1] = lax.optimization_barrier((turned, parts[-1][1]))
        parts.append(exchange(turned, "layer"))
    (padded,) = call(
        pad_kernel,
        [(LANES // block_rows * weights, LANES, slice_rows)],
        [],
        jnp.swapaxes(table, 1, 2),
        after=before,
    )

    received, before = [], ()
    for h in range(halves):
        shares = call(
            functools.partial(pupil_kernel, n_layer, n_row, entries, entries),
            [(each, points)] * n_row,
            [
                pltpu.VMEM((n_row * owned, each, slice_rows), F32),
                pltpu.VMEM((n_layer * CODE_ROWS, LANES), jnp.int32),
                pltpu.SMEM((n_layer * CODE_ROWS, LANES), jnp.int32),
                pltpu.SemaphoreType.DMA,
            ],
            padded,
            *parts[0],
            *parts[h],
            after=before,
        )
        before = (shares[0],)
        if h > 0:
            shares, received[-1] = lax.optimization_barrier((shares, received[-1]))
        received.append(exchange(shares, "row"))
    results, ahead = [], tuple(received[-1][1:2])
    for h in range(halves):
        (pupil,) = call(sum_kernel, [(each, points)], [], *received[h], after=before)
        pieces = gather(pupil, "layer", h == 0)
        partial = call(
            functools.partial(fit_kernel, n_layer, n_row),
            [(chunk // halves, actuators)] * n_row,
            [pltpu.VMEM((n_layer, each, points), BF16), pltpu.VMEM((per_half, actuators), F32)],
            fitting.T,
            *pieces,
            after=ahead,
        )
        before = (partial[0],)
        results.append(exchange(partial, "row"))
        ahead = tuple(results[-1][1:2])
    return jnp.concatenate([total_of(result) for result in results], 0)


def solution(mesh):
    return jax.shard_map(
        local,
        mesh=mesh,
        in_specs=(
            P("layer", "row", "panel"),
            P(),
            P("row", "layer"),
            P("layer", "row", None),
            P("layer", "row"),
            P("layer", "row"),
            P("layer", "row"),
        ),
        out_specs=P(("panel", "row"), "layer"),
        check_vma=False,
    )
```

```python
import functools

import jax
import jax.numpy as jnp
from jax import lax
from jax.experimental import pallas as pl
from jax.experimental.pallas import tpu as pltpu
from jax.sharding import PartitionSpec as P

LANES = 128
CODE_ROWS = 16
F32, BF16 = jnp.float32, jnp.bfloat16
VMEM = pl.BlockSpec(memory_space=pltpu.VMEM)
ANY = pl.BlockSpec(memory_space=pl.ANY)
PARAMS = dict(vmem_limit_bytes=16 * 1024 * 1024)


def turn_kernel(n_layer, n_row, halves, half, layers_ref, extra_ref, *refs):
    outs, codes = refs[:n_layer], refs[-1]
    rows_dev, columns = layers_ref.shape
    per_half = columns // halves
    each = per_half // n_layer
    chunk, part = columns // n_row, columns // n_row // halves
    me = lax.axis_index("layer")
    row = lax.broadcasted_iota(jnp.int32, (per_half, columns), 0)
    col = lax.broadcasted_iota(jnp.int32, (per_half, columns), 1)
    place = lax.bitwise_xor(row // each, me) * each + lax.rem(row, each)
    wanted = (place // part) * chunk + lax.rem(place, part) + half * part
    pick = (col == wanted).astype(BF16)
    turned = lax.dot_general(
        pick, layers_ref[...], (((1,), (1,)), ((), ())), preferred_element_type=F32
    ).astype(BF16)
    for i, out in enumerate(outs):
        k = (n_layer - i) % n_layer
        out[:, :rows_dev] = turned[k * each : (k + 1) * each]
    if half == 0:
        codes[...] = jnp.zeros_like(codes)
        codes[: extra_ref.shape[0], : extra_ref.shape[1]] = extra_ref[...]
        tail = codes[...].astype(F32).astype(BF16)
        for out in outs:
            out[:, rows_dev:] = jnp.zeros((each, LANES), BF16)
            out[:CODE_ROWS, rows_dev:] = tail


def pad_kernel(table_ref, padded):
    weights, block_rows = table_ref.shape[:2]
    padded[...] = jnp.zeros_like(padded)
    for half in range(LANES // block_rows):
        start = half * block_rows
        padded[half * weights : (half + 1) * weights, start : start + block_rows] = table_ref[...]


def pupil_kernel(n_layer, n_row, entries, unroll, padded, *refs):
    coded, parts = refs[:n_layer], refs[n_layer : 2 * n_layer]
    outs = refs[2 * n_layer : 2 * n_layer + n_row]
    total, codes, code, sem = refs[-4:]
    weights = padded.shape[0] // 2
    owned = outs[0].shape[1] // LANES
    for j, ref in enumerate(coded):
        tail = ref[:CODE_ROWS, ref.shape[1] - LANES :]
        codes[j * CODE_ROWS : (j + 1) * CODE_ROWS] = tail.astype(F32).astype(jnp.int32)
    copy = pltpu.make_async_copy(codes, code, sem)
    copy.start()
    total[...] = jnp.zeros_like(total)
    copy.wait()
    for j, part in enumerate(parts):
        base = j * CODE_ROWS

        def step(group, carry):
            terms = []
            for u in range(unroll):
                e = group * unroll + u
                block = code[base + 2, e]
                source = part[:, pl.ds(pl.multiple_of((block // 2) * LANES, LANES), LANES)]
                weight = padded[lax.rem(block, 2) * weights + code[base + 3, e]]
                dest = code[base, e] * owned + code[base + 1, e]
                terms.append((dest, jnp.dot(source, weight, preferred_element_type=F32)))
            for dest, term in terms:
                total[dest] += term
            return carry

        lax.fori_loop(0, entries // unroll, step, 0)
    me = lax.axis_index("row")
    for i, out in enumerate(outs):
        k = (n_row - i) % n_row
        base = lax.bitwise_xor(me, k) * owned
        for s in range(owned):
            out[:, s * LANES : (s + 1) * LANES] = total[base + s].astype(BF16)


def sum_kernel(count, *refs):
    found = sum(ref[...].astype(F32) for ref in refs[:count]).astype(BF16)
    start = 0
    for i, out in enumerate(refs[count:]):
        rows = out.shape[0]
        out[...] = found[start : start + rows]
        start = 0 if i == 0 else start + rows


def fit_kernel(places, n_row, fitting_ref, *refs):
    pieces, outs = refs[: len(places)], refs[len(places) : len(places) + n_row]
    left, product = refs[-2], refs[-1]
    aligned = left.shape[0] == n_row
    me, row = lax.axis_index("layer"), lax.axis_index("row")
    for piece, spots in zip(pieces, places):
        for k, of, to, count in spots:
            place = lax.bitwise_xor(me, k)
            place = lax.bitwise_xor(place, row) if aligned else place
            left[place, to : to + count] = piece[of : of + count]
    columns = left.shape[0] * left.shape[1]
    found = lax.dot_general(
        left[...].reshape(columns, left.shape[2]),
        fitting_ref[...],
        (((1,), (1,)), ((), ())),
        preferred_element_type=F32,
    )
    each = columns // n_row
    if aligned:
        for i, out in enumerate(outs):
            k = (n_row - i) % n_row
            out[...] = found[k * each : (k + 1) * each].astype(BF16)
    else:
        product[...] = found
        for i, out in enumerate(outs):
            k = (n_row - i) % n_row
            start = pl.multiple_of(lax.bitwise_xor(row, k) * each, each)
            out[...] = product[pl.ds(start, each), :].astype(BF16)


def trade(chunk, axis, k):
    return lax.ppermute(chunk, axis, [(j, j ^ k) for j in range(lax.axis_size(axis))])


def exchange(chunks, axis):
    n = len(chunks)
    return [trade(chunk, axis, n - i) if i else chunk for i, chunk in enumerate(chunks)]


def gather(piece, axis, paired):
    got, n, rows = [piece], lax.axis_size(axis), piece.shape[0]
    for k in range(1, n):
        got.append(trade(got[k - 1], axis, 1) if paired and k % 2 else trade(piece, axis, k))
    return got, [[(k, 0, 0, rows)] for k in range(n)]


def gather_crossed(piece, first, second, axis, ahead):
    rows, half = piece.shape[0], first.shape[0]
    got = [piece, trade(piece, axis, 1)]
    places = [[(0, 0, 0, rows)], [(1, 0, 0, rows)]]
    for k in range(2, lax.axis_size(axis), 2):
        upper, lower = trade(first, axis, k), trade(second, axis, k + 1)
        upper, ahead = lax.optimization_barrier((upper, ahead))
        got += [upper, lower, trade(jnp.concatenate([upper, lower], 0), axis, 1)]
        places += [[(k, 0, 0, half)], [(k + 1, 0, half, half)]]
        places.append([(k + 1, 0, 0, half), (k, half, half, half)])
    return got, places


def total_of(parts):
    return sum(part.astype(F32) for part in parts).astype(BF16)


def call(kernel, shapes, scratch, *args, after=()):
    given = len(args)

    def body(*refs):
        kernel(*refs[:given], *refs[given + len(after) :])

    return pl.pallas_call(
        body,
        out_shape=[jax.ShapeDtypeStruct(shape, BF16) for shape in shapes],
        in_specs=[VMEM] * len(args) + [ANY] * len(after),
        out_specs=[VMEM] * len(shapes),
        scratch_shapes=scratch,
        compiler_params=pltpu.CompilerParams(**PARAMS),
    )(*args, *after)


def local(layers, table, fitting, owner, local_slice, block_index, weight_index):
    n_layer, n_row = lax.axis_size("layer"), lax.axis_size("row")
    rows_dev, columns = layers.shape[1:]
    entries = owner.shape[1]
    weights, slice_rows, block_rows = table.shape
    points, actuators = fitting.shape
    owned = points // slice_rows
    chunk = columns // n_row
    halves = 2 if chunk % 32 == 0 else 1
    per_half = columns // halves
    each = per_half // n_layer

    indices = jnp.concatenate([owner[:, :, 0], local_slice, block_index, weight_index], 0)
    parts, before = [], ()
    for h in range(halves):
        turned = call(
            functools.partial(turn_kernel, n_layer, n_row, halves, h),
            [(each, rows_dev + (LANES if h == 0 else 0))] * n_layer,
            [pltpu.VMEM((CODE_ROWS, LANES), jnp.int32)],
            layers[0],
            indices,
            after=before,
        )
        before = (turned[0],)
        if h == 0:
            (padded,) = call(
                pad_kernel,
                [(LANES // block_rows * weights, LANES, slice_rows)],
                [],
                jnp.swapaxes(table, 1, 2),
                after=before,
            )
        else:
            turned, parts[-1][1], padded = lax.optimization_barrier((turned, parts[-1][1], padded))
        parts.append(exchange(turned, "layer"))

    received, before = [], ()
    for h in range(halves):
        shares = call(
            functools.partial(pupil_kernel, n_layer, n_row, entries, entries),
            [(each, points)] * n_row,
            [
                pltpu.VMEM((n_row * owned, each, slice_rows), F32),
                pltpu.VMEM((n_layer * CODE_ROWS, LANES), jnp.int32),
                pltpu.SMEM((n_layer * CODE_ROWS, LANES), jnp.int32),
                pltpu.SemaphoreType.DMA,
            ],
            padded,
            *parts[0],
            *parts[h],
            after=before,
        )
        before = (shares[0],)
        if h > 0:
            shares, received[-1] = lax.optimization_barrier((shares, received[-1]))
        received.append(exchange(shares, "row"))
    results, ahead = [], tuple(received[-1][1:2])
    for h in range(halves):
        shapes = [(each, points)] + [(each // 2, points)] * 2 * (h > 0)
        pupil = call(functools.partial(sum_kernel, n_row), shapes, [], *received[h], after=before)
        if h > 0:
            pieces, places = gather_crossed(*pupil, "layer", ahead)
        else:
            pieces, places = gather(*pupil, "layer", True)
        partial = call(
            functools.partial(fit_kernel, places, n_row),
            [(chunk // halves, actuators)] * n_row,
            [pltpu.VMEM((n_layer, each, points), BF16), pltpu.VMEM((per_half, actuators), F32)],
            fitting.T,
            *pieces,
            after=ahead if h == 0 else (),
        )
        before = (partial[0],)
        results.append(exchange(partial, "row"))
        ahead = results[-1][1]
    return jnp.concatenate([total_of(result) for result in results], 0)


def solution(mesh):
    return jax.shard_map(
        local,
        mesh=mesh,
        in_specs=(
            P("layer", "row", "panel"),
            P(),
            P("row", "layer"),
            P("layer", "row", None),
            P("layer", "row"),
            P("layer", "row"),
            P("layer", "row"),
        ),
        out_specs=P(("panel", "row"), "layer"),
        check_vma=False,
    )
```

```python
import functools

import jax
import jax.numpy as jnp
from jax import lax
from jax.experimental import pallas as pl
from jax.experimental.pallas import tpu as pltpu
from jax.sharding import PartitionSpec as P

LANES = 128
CODE_ROWS = 16
F32, BF16 = jnp.float32, jnp.bfloat16
VMEM = pl.BlockSpec(memory_space=pltpu.VMEM)
ANY = pl.BlockSpec(memory_space=pl.ANY)
PARAMS = dict(vmem_limit_bytes=16 * 1024 * 1024)


def turn_kernel(n_layer, n_row, halves, half, layers_ref, extra_ref, *refs):
    outs, codes = refs[:n_layer], refs[-1]
    rows_dev, columns = layers_ref.shape
    per_half = columns // halves
    each = per_half // n_layer
    chunk, part = columns // n_row, columns // n_row // halves
    me = lax.axis_index("layer")
    row = lax.broadcasted_iota(jnp.int32, (per_half, columns), 0)
    col = lax.broadcasted_iota(jnp.int32, (per_half, columns), 1)
    place = lax.bitwise_xor(row // each, me) * each + lax.rem(row, each)
    wanted = (place // part) * chunk + lax.rem(place, part) + half * part
    pick = (col == wanted).astype(BF16)
    turned = lax.dot_general(
        pick, layers_ref[...], (((1,), (1,)), ((), ())), preferred_element_type=F32
    ).astype(BF16)
    for i, out in enumerate(outs):
        k = (n_layer - i) % n_layer
        out[:, :rows_dev] = turned[k * each : (k + 1) * each]
    if half == 0:
        codes[...] = jnp.zeros_like(codes)
        codes[: extra_ref.shape[0], : extra_ref.shape[1]] = extra_ref[...]
        tail = codes[...].astype(F32).astype(BF16)
        for out in outs:
            out[:, rows_dev:] = jnp.zeros((each, LANES), BF16)
            out[:CODE_ROWS, rows_dev:] = tail


def pad_kernel(table_ref, padded):
    weights, block_rows = table_ref.shape[:2]
    padded[...] = jnp.zeros_like(padded)
    for half in range(LANES // block_rows):
        start = half * block_rows
        padded[half * weights : (half + 1) * weights, start : start + block_rows] = table_ref[...]


def pupil_kernel(n_layer, n_row, entries, unroll, padded, *refs):
    coded, parts = refs[:n_layer], refs[n_layer : 2 * n_layer]
    outs = refs[2 * n_layer : 2 * n_layer + n_row]
    total, codes, code, sem = refs[-4:]
    weights = padded.shape[0] // 2
    owned = outs[0].shape[1] // LANES
    for j, ref in enumerate(coded):
        tail = ref[:CODE_ROWS, ref.shape[1] - LANES :]
        codes[j * CODE_ROWS : (j + 1) * CODE_ROWS] = tail.astype(F32).astype(jnp.int32)
    copy = pltpu.make_async_copy(codes, code, sem)
    copy.start()
    total[...] = jnp.zeros_like(total)
    copy.wait()
    for j, part in enumerate(parts):
        base = j * CODE_ROWS

        def step(group, carry):
            terms = []
            for u in range(unroll):
                e = group * unroll + u
                block = code[base + 2, e]
                source = part[:, pl.ds(pl.multiple_of((block // 2) * LANES, LANES), LANES)]
                weight = padded[lax.rem(block, 2) * weights + code[base + 3, e]]
                dest = code[base, e] * owned + code[base + 1, e]
                terms.append((dest, jnp.dot(source, weight, preferred_element_type=F32)))
            for dest, term in terms:
                total[dest] += term
            return carry

        lax.fori_loop(0, entries // unroll, step, 0)
    me = lax.axis_index("row")
    for i, out in enumerate(outs):
        k = (n_row - i) % n_row
        base = lax.bitwise_xor(me, k) * owned
        for s in range(owned):
            out[:, s * LANES : (s + 1) * LANES] = total[base + s].astype(BF16)


def sum_kernel(*refs):
    refs[-1][...] = sum(ref[...].astype(F32) for ref in refs[:-1]).astype(BF16)


def fit_kernel(n_layer, n_row, fitting_ref, *refs):
    pieces, outs = refs[:n_layer], refs[n_layer : n_layer + n_row]
    left, product = refs[-2], refs[-1]
    aligned = n_layer == n_row
    me, row = lax.axis_index("layer"), lax.axis_index("row")
    for j, piece in enumerate(pieces):
        place = lax.bitwise_xor(me, (j + 1) % n_layer)
        left[lax.bitwise_xor(place, row) if aligned else place] = piece[...]
    columns = left.shape[0] * left.shape[1]
    found = lax.dot_general(
        left[...].reshape(columns, left.shape[2]),
        fitting_ref[...],
        (((1,), (1,)), ((), ())),
        preferred_element_type=F32,
    )
    each = columns // n_row
    if aligned:
        for i, out in enumerate(outs):
            k = (n_row - i) % n_row
            out[...] = found[k * each : (k + 1) * each].astype(BF16)
    else:
        product[...] = found
        for i, out in enumerate(outs):
            k = (n_row - i) % n_row
            start = pl.multiple_of(lax.bitwise_xor(row, k) * each, each)
            out[...] = product[pl.ds(start, each), :].astype(BF16)


def trade(chunk, axis, k):
    return lax.ppermute(chunk, axis, [(j, j ^ k) for j in range(lax.axis_size(axis))])


def exchange(chunks, axis):
    n = len(chunks)
    return [trade(chunk, axis, n - i) if i else chunk for i, chunk in enumerate(chunks)]


def total_of(parts):
    return sum(part.astype(F32) for part in parts).astype(BF16)


def call(kernel, shapes, scratch, *args, after=()):
    given = len(args)

    def body(*refs):
        kernel(*refs[:given], *refs[given + len(after) :])

    return pl.pallas_call(
        body,
        out_shape=[jax.ShapeDtypeStruct(shape, BF16) for shape in shapes],
        in_specs=[VMEM] * len(args) + [ANY] * len(after),
        out_specs=[VMEM] * len(shapes),
        scratch_shapes=scratch,
        compiler_params=pltpu.CompilerParams(**PARAMS),
    )(*args, *after)


def local(layers, table, fitting, owner, local_slice, block_index, weight_index):
    n_layer, n_row = lax.axis_size("layer"), lax.axis_size("row")
    rows_dev, columns = layers.shape[1:]
    entries = owner.shape[1]
    weights, slice_rows, block_rows = table.shape
    points, actuators = fitting.shape
    owned = points // slice_rows
    chunk = columns // n_row
    halves = 2 if chunk % 32 == 0 else 1
    per_half = columns // halves
    each = per_half // n_layer

    indices = jnp.concatenate([owner[:, :, 0], local_slice, block_index, weight_index], 0)
    parts, before = [], ()
    for h in range(halves):
        turned = call(
            functools.partial(turn_kernel, n_layer, n_row, halves, h),
            [(each, rows_dev + (LANES if h == 0 else 0))] * n_layer,
            [pltpu.VMEM((CODE_ROWS, LANES), jnp.int32)],
            layers[0],
            indices,
            after=before,
        )
        before = (turned[0],)
        if h == 0:
            (padded,) = call(
                pad_kernel,
                [(LANES // block_rows * weights, LANES, slice_rows)],
                [],
                jnp.swapaxes(table, 1, 2),
                after=before,
            )
        else:
            turned, parts[-1][1], padded = lax.optimization_barrier((turned, parts[-1][1], padded))
        parts.append(exchange(turned, "layer"))

    received, before = [], ()
    for h in range(halves):
        shares = call(
            functools.partial(pupil_kernel, n_layer, n_row, entries, entries),
            [(each, points)] * n_row,
            [
                pltpu.VMEM((n_row * owned, each, slice_rows), F32),
                pltpu.VMEM((n_layer * CODE_ROWS, LANES), jnp.int32),
                pltpu.SMEM((n_layer * CODE_ROWS, LANES), jnp.int32),
                pltpu.SemaphoreType.DMA,
            ],
            padded,
            *parts[0],
            *parts[h],
            after=before,
        )
        before = (shares[0],)
        if h > 0:
            shares, received[-1] = lax.optimization_barrier((shares, received[-1]))
        received.append(exchange(shares, "row"))
    pupils = []
    for h in range(halves):
        pupils += call(sum_kernel, [(each, points)], [], *received[h], after=before)
    results = []
    for h in range(halves):
        pieces = exchange([pupils[h]] * n_layer, "layer")[::-1]
        partial = call(
            functools.partial(fit_kernel, n_layer, n_row),
            [(chunk // halves, actuators)] * n_row,
            [pltpu.VMEM((n_layer, each, points), BF16), pltpu.VMEM((per_half, actuators), F32)],
            fitting.T,
            *pieces,
            after=pupils[h + 1 :],
        )
        results.append(exchange(partial, "row"))
    return jnp.concatenate([total_of(result) for result in results], 0)


def solution(mesh):
    return jax.shard_map(
        local,
        mesh=mesh,
        in_specs=(
            P("layer", "row", "panel"),
            P(),
            P("row", "layer"),
            P("layer", "row", None),
            P("layer", "row"),
            P("layer", "row"),
            P("layer", "row"),
        ),
        out_specs=P(("panel", "row"), "layer"),
        check_vma=False,
    )
```

```python
import functools

import jax
import jax.numpy as jnp
from jax import lax
from jax.experimental import pallas as pl
from jax.experimental.pallas import tpu as pltpu
from jax.sharding import PartitionSpec as P

LANES = 128
CODE_ROWS = 16
F32, BF16 = jnp.float32, jnp.bfloat16
VMEM = pl.BlockSpec(memory_space=pltpu.VMEM)
ANY = pl.BlockSpec(memory_space=pl.ANY)
PARAMS = dict(vmem_limit_bytes=16 * 1024 * 1024)


def turn_kernel(n_layer, n_row, halves, half, layers_ref, extra_ref, *refs):
    outs, codes = refs[:n_layer], refs[-1]
    rows_dev, columns = layers_ref.shape
    per_half = columns // halves
    each = per_half // n_layer
    chunk, part = columns // n_row, columns // n_row // halves
    me = lax.axis_index("layer")
    row = lax.broadcasted_iota(jnp.int32, (per_half, columns), 0)
    col = lax.broadcasted_iota(jnp.int32, (per_half, columns), 1)
    place = lax.bitwise_xor(row // each, me) * each + lax.rem(row, each)
    wanted = (place // part) * chunk + lax.rem(place, part) + half * part
    pick = (col == wanted).astype(BF16)
    turned = lax.dot_general(
        pick, layers_ref[...], (((1,), (1,)), ((), ())), preferred_element_type=F32
    ).astype(BF16)
    for i, out in enumerate(outs):
        k = (n_layer - i) % n_layer
        out[:, :rows_dev] = turned[k * each : (k + 1) * each]
    if half == 0:
        codes[...] = jnp.zeros_like(codes)
        codes[: extra_ref.shape[0], : extra_ref.shape[1]] = extra_ref[...]
        tail = codes[...].astype(F32).astype(BF16)
        for out in outs:
            out[:, rows_dev:] = jnp.zeros((each, LANES), BF16)
            out[:CODE_ROWS, rows_dev:] = tail


def pad_kernel(table_ref, padded):
    weights, block_rows = table_ref.shape[:2]
    padded[...] = jnp.zeros_like(padded)
    for half in range(LANES // block_rows):
        start = half * block_rows
        padded[half * weights : (half + 1) * weights, start : start + block_rows] = table_ref[...]


def pupil_kernel(n_layer, n_row, entries, unroll, padded, *refs):
    coded, parts = refs[:n_layer], refs[n_layer : 2 * n_layer]
    outs = refs[2 * n_layer : 2 * n_layer + n_row]
    total, codes, code, sem = refs[-4:]
    weights = padded.shape[0] // 2
    owned = outs[0].shape[1] // LANES
    for j, ref in enumerate(coded):
        tail = ref[:CODE_ROWS, ref.shape[1] - LANES :]
        codes[j * CODE_ROWS : (j + 1) * CODE_ROWS] = tail.astype(F32).astype(jnp.int32)
    copy = pltpu.make_async_copy(codes, code, sem)
    copy.start()
    total[...] = jnp.zeros_like(total)
    copy.wait()
    for j, part in enumerate(parts):
        base = j * CODE_ROWS

        def step(group, carry):
            terms = []
            for u in range(unroll):
                e = group * unroll + u
                block = code[base + 2, e]
                source = part[:, pl.ds(pl.multiple_of((block // 2) * LANES, LANES), LANES)]
                weight = padded[lax.rem(block, 2) * weights + code[base + 3, e]]
                dest = code[base, e] * owned + code[base + 1, e]
                terms.append((dest, jnp.dot(source, weight, preferred_element_type=F32)))
            for dest, term in terms:
                total[dest] += term
            return carry

        lax.fori_loop(0, entries // unroll, step, 0)
    me = lax.axis_index("row")
    for i, out in enumerate(outs):
        k = (n_row - i) % n_row
        base = lax.bitwise_xor(me, k) * owned
        for s in range(owned):
            out[:, s * LANES : (s + 1) * LANES] = total[base + s].astype(BF16)


def sum_kernel(*refs):
    refs[-1][...] = sum(ref[...].astype(F32) for ref in refs[:-1]).astype(BF16)


def fit_kernel(n_layer, n_row, fitting_ref, *refs):
    pieces, outs = refs[:n_layer], refs[n_layer : n_layer + n_row]
    left, product = refs[-2], refs[-1]
    aligned = n_layer == n_row
    me, row = lax.axis_index("layer"), lax.axis_index("row")
    for j, piece in enumerate(pieces):
        place = lax.bitwise_xor(me, (j + 1) % n_layer)
        left[lax.bitwise_xor(place, row) if aligned else place] = piece[...]
    columns = left.shape[0] * left.shape[1]
    found = lax.dot_general(
        left[...].reshape(columns, left.shape[2]),
        fitting_ref[...],
        (((1,), (1,)), ((), ())),
        preferred_element_type=F32,
    )
    each = columns // n_row
    if aligned:
        for i, out in enumerate(outs):
            k = (n_row - i) % n_row
            out[...] = found[k * each : (k + 1) * each].astype(BF16)
    else:
        product[...] = found
        for i, out in enumerate(outs):
            k = (n_row - i) % n_row
            start = pl.multiple_of(lax.bitwise_xor(row, k) * each, each)
            out[...] = product[pl.ds(start, each), :].astype(BF16)


def trade(chunk, axis, k):
    return lax.ppermute(chunk, axis, [(j, j ^ k) for j in range(lax.axis_size(axis))])


def exchange(chunks, axis):
    n = len(chunks)
    return [trade(chunk, axis, n - i) if i else chunk for i, chunk in enumerate(chunks)]


def total_of(parts):
    return sum(part.astype(F32) for part in parts).astype(BF16)


def call(kernel, shapes, scratch, *args, after=(), fused=None):
    given = len(args)

    def body(*refs):
        kernel(*refs[:given], *refs[given + len(after) :])

    return pl.pallas_call(
        body,
        out_shape=[jax.ShapeDtypeStruct(shape, BF16) for shape in shapes],
        in_specs=[VMEM] * len(args) + [ANY] * len(after),
        out_specs=[VMEM] * len(shapes),
        scratch_shapes=scratch,
        compiler_params=pltpu.CompilerParams(allow_input_fusion=fused, **PARAMS),
    )(*args, *after)


def local(layers, table, fitting, owner, local_slice, block_index, weight_index):
    n_layer, n_row = lax.axis_size("layer"), lax.axis_size("row")
    rows_dev, columns = layers.shape[1:]
    entries = owner.shape[1]
    weights, slice_rows, block_rows = table.shape
    points, actuators = fitting.shape
    owned = points // slice_rows
    chunk = columns // n_row
    halves = 2 if chunk % 32 == 0 else 1
    per_half = columns // halves
    each = per_half // n_layer

    indices = jnp.concatenate([owner[:, :, 0], local_slice, block_index, weight_index], 0)
    parts, before = [], ()
    for h in range(halves):
        turned = call(
            functools.partial(turn_kernel, n_layer, n_row, halves, h),
            [(each, rows_dev + (LANES if h == 0 else 0))] * n_layer,
            [pltpu.VMEM((CODE_ROWS, LANES), jnp.int32)],
            layers[0],
            indices if h == 0 else before[0],
            after=before,
            fused=None if h else [False, True],
        )
        before = (turned[0],)
        if h == 0:
            (padded,) = call(
                pad_kernel,
                [(LANES // block_rows * weights, LANES, slice_rows)],
                [],
                jnp.swapaxes(table, 1, 2),
                after=before,
            )
        else:
            turned, parts[-1][1], padded = lax.optimization_barrier((turned, parts[-1][1], padded))
        parts.append(exchange(turned, "layer"))

    received, before = [], ()
    for h in range(halves):
        shares = call(
            functools.partial(pupil_kernel, n_layer, n_row, entries, entries),
            [(each, points)] * n_row,
            [
                pltpu.VMEM((n_row * owned, each, slice_rows), F32),
                pltpu.VMEM((n_layer * CODE_ROWS, LANES), jnp.int32),
                pltpu.SMEM((n_layer * CODE_ROWS, LANES), jnp.int32),
                pltpu.SemaphoreType.DMA,
            ],
            padded,
            *parts[0],
            *parts[h],
            after=before,
        )
        before = (shares[0],)
        if h > 0:
            shares, received[-1] = lax.optimization_barrier((shares, received[-1]))
        received.append(exchange(shares, "row"))
    pupils = []
    for h in range(halves):
        pupils += call(sum_kernel, [(each, points)], [], *received[h], after=before)
    results = []
    for h in range(halves):
        pieces = exchange([pupils[h]] * n_layer, "layer")[::-1]
        partial = call(
            functools.partial(fit_kernel, n_layer, n_row),
            [(chunk // halves, actuators)] * n_row,
            [pltpu.VMEM((n_layer, each, points), BF16), pltpu.VMEM((per_half, actuators), F32)],
            fitting.T,
            *pieces,
            after=pupils[h + 1 :],
        )
        results.append(exchange(partial, "row"))
    return jnp.concatenate([total_of(result) for result in results], 0)


def solution(mesh):
    return jax.shard_map(
        local,
        mesh=mesh,
        in_specs=(
            P("layer", "row", "panel"),
            P(),
            P("row", "layer"),
            P("layer", "row", None),
            P("layer", "row"),
            P("layer", "row"),
            P("layer", "row"),
        ),
        out_specs=P(("panel", "row"), "layer"),
        check_vma=False,
    )
```

```python
import functools

import jax
import jax.numpy as jnp
from jax import lax
from jax.experimental import pallas as pl
from jax.experimental.pallas import tpu as pltpu
from jax.sharding import PartitionSpec as P

LANES = 128
CODE_ROWS = 16
F32, BF16 = jnp.float32, jnp.bfloat16
VMEM = pl.BlockSpec(memory_space=pltpu.VMEM)
ANY = pl.BlockSpec(memory_space=pl.ANY)
PARAMS = dict(vmem_limit_bytes=16 * 1024 * 1024)


def turn_kernel(n_layer, n_row, halves, half, layers_ref, extra_ref, *refs):
    outs, codes = refs[:n_layer], refs[-1]
    rows_dev, columns = layers_ref.shape
    per_half = columns // halves
    each = per_half // n_layer
    chunk, part = columns // n_row, columns // n_row // halves
    me = lax.axis_index("layer")
    row = lax.broadcasted_iota(jnp.int32, (per_half, columns), 0)
    col = lax.broadcasted_iota(jnp.int32, (per_half, columns), 1)
    place = lax.bitwise_xor(row // each, me) * each + lax.rem(row, each)
    wanted = (place // part) * chunk + lax.rem(place, part) + half * part
    pick = (col == wanted).astype(BF16)
    turned = lax.dot_general(
        pick, layers_ref[...], (((1,), (1,)), ((), ())), preferred_element_type=F32
    ).astype(BF16)
    for i, out in enumerate(outs):
        k = (n_layer - i) % n_layer
        out[:, :rows_dev] = turned[k * each : (k + 1) * each]
    if half == 0:
        codes[...] = jnp.zeros_like(codes)
        codes[: extra_ref.shape[0], : extra_ref.shape[1]] = extra_ref[...]
        tail = codes[...].astype(F32).astype(BF16)
        for out in outs:
            out[:, rows_dev:] = jnp.zeros((each, LANES), BF16)
            out[:CODE_ROWS, rows_dev:] = tail


def near_kernel(table_ref, near):
    near[...] = table_ref[...]


def pupil_kernel(n_layer, n_row, entries, block_rows, near, *refs):
    coded, parts = refs[:n_layer], refs[n_layer : 2 * n_layer]
    outs = refs[2 * n_layer : 2 * n_layer + n_row]
    total, codes, code, shifted, sem = refs[-5:]
    packed = LANES // block_rows
    owned = outs[0].shape[1] // LANES
    for j, ref in enumerate(coded):
        tail = ref[:CODE_ROWS, ref.shape[1] - LANES :]
        codes[j * CODE_ROWS : (j + 1) * CODE_ROWS] = tail.astype(F32).astype(jnp.int32)
    copy = pltpu.make_async_copy(codes, code, sem)
    copy.start()
    total[...] = jnp.zeros_like(total)
    for j, part in enumerate(parts):
        rows = shifted.shape[3]
        found = part[:, :rows].astype(F32)
        for p in range(packed):
            moved = pltpu.roll(found, rows - p * block_rows, 1) if p else found
            shifted[j, p] = moved.astype(BF16)
    copy.wait()
    for j in range(n_layer):
        base, terms = j * CODE_ROWS, []
        for e in range(entries):
            block = code[base + 2, e]
            lanes = pl.ds(pl.multiple_of((block // packed) * LANES, LANES), LANES)
            source = shifted[j, lax.rem(block, packed), :, lanes][:, :block_rows]
            weight = near[code[base + 3, e]]
            dest = code[base, e] * owned + code[base + 1, e]
            terms.append((dest, jnp.dot(source, weight, preferred_element_type=F32)))
        for dest, term in terms:
            total[dest] += term
    me = lax.axis_index("row")
    for i, out in enumerate(outs):
        k = (n_row - i) % n_row
        base = lax.bitwise_xor(me, k) * owned
        for s in range(owned):
            out[:, s * LANES : (s + 1) * LANES] = total[base + s].astype(BF16)


def sum_kernel(*refs):
    refs[-1][...] = sum(ref[...].astype(F32) for ref in refs[:-1]).astype(BF16)


def finish_kernel(*refs):
    parts, out = refs[:-1], refs[-1]
    rows = parts[0].shape[0]
    halves = out.shape[0] // rows
    each = len(parts) // halves
    for h in range(halves):
        found = sum(part[...].astype(F32) for part in parts[h * each : (h + 1) * each])
        out[h * rows : (h + 1) * rows] = found.astype(BF16)


def fit_kernel(n_layer, n_row, fitting_ref, *refs):
    pieces, outs = refs[:n_layer], refs[n_layer : n_layer + n_row]
    left, product = refs[-2], refs[-1]
    aligned = n_layer == n_row
    me, row = lax.axis_index("layer"), lax.axis_index("row")
    for j, piece in enumerate(pieces):
        place = lax.bitwise_xor(me, (j + 1) % n_layer)
        left[lax.bitwise_xor(place, row) if aligned else place] = piece[...]
    columns = left.shape[0] * left.shape[1]
    found = lax.dot_general(
        left[...].reshape(columns, left.shape[2]),
        fitting_ref[...],
        (((1,), (1,)), ((), ())),
        preferred_element_type=F32,
    )
    each = columns // n_row
    if aligned:
        for i, out in enumerate(outs):
            k = (n_row - i) % n_row
            out[...] = found[k * each : (k + 1) * each].astype(BF16)
    else:
        product[...] = found
        for i, out in enumerate(outs):
            k = (n_row - i) % n_row
            start = pl.multiple_of(lax.bitwise_xor(row, k) * each, each)
            out[...] = product[pl.ds(start, each), :].astype(BF16)


def trade(chunk, axis, k):
    return lax.ppermute(chunk, axis, [(j, j ^ k) for j in range(lax.axis_size(axis))])


def exchange(chunks, axis):
    n = len(chunks)
    return [trade(chunk, axis, n - i) if i else chunk for i, chunk in enumerate(chunks)]


def call(kernel, shapes, scratch, *args, after=()):
    given = len(args)

    def body(*refs):
        kernel(*refs[:given], *refs[given + len(after) :])

    return pl.pallas_call(
        body,
        out_shape=[jax.ShapeDtypeStruct(shape, BF16) for shape in shapes],
        in_specs=[VMEM] * len(args) + [ANY] * len(after),
        out_specs=[VMEM] * len(shapes),
        scratch_shapes=scratch,
        compiler_params=pltpu.CompilerParams(**PARAMS),
    )(*args, *after)


def local(layers, table, fitting, owner, local_slice, block_index, weight_index):
    n_layer, n_row = lax.axis_size("layer"), lax.axis_size("row")
    rows_dev, columns = layers.shape[1:]
    entries = owner.shape[1]
    weights, slice_rows, block_rows = table.shape
    points, actuators = fitting.shape
    owned = points // slice_rows
    chunk = columns // n_row
    halves = 2 if chunk % 32 == 0 else 1
    per_half = columns // halves
    each = per_half // n_layer

    indices = jnp.concatenate([owner[:, :, 0], local_slice, block_index, weight_index], 0)
    parts, before = [], ()
    for h in range(halves):
        turned = call(
            functools.partial(turn_kernel, n_layer, n_row, halves, h),
            [(each, rows_dev + (LANES if h == 0 else 0))] * n_layer,
            [pltpu.VMEM((CODE_ROWS, LANES), jnp.int32)],
            layers[0],
            indices,
            after=before,
        )
        before = (turned[0],)
        if h == 0:
            (near,) = call(
                near_kernel,
                [(weights, block_rows, slice_rows)],
                [],
                jnp.swapaxes(table, 1, 2),
                after=before,
            )
        else:
            turned, parts[-1][1], near = lax.optimization_barrier((turned, parts[-1][1], near))
        parts.append(exchange(turned, "layer"))

    received, before = [], ()
    for h in range(halves):
        shares = call(
            functools.partial(pupil_kernel, n_layer, n_row, entries, block_rows),
            [(each, points)] * n_row,
            [
                pltpu.VMEM((n_row * owned, each, slice_rows), F32),
                pltpu.VMEM((n_layer * CODE_ROWS, LANES), jnp.int32),
                pltpu.SMEM((n_layer * CODE_ROWS, LANES), jnp.int32),
                pltpu.VMEM((n_layer, LANES // block_rows, each, rows_dev), BF16),
                pltpu.SemaphoreType.DMA,
            ],
            near,
            *parts[0],
            *parts[h],
            after=before,
        )
        before = (shares[0],)
        if h > 0:
            shares, received[-1] = lax.optimization_barrier((shares, received[-1]))
        received.append(exchange(shares, "row"))
    pupils = []
    for h in range(halves):
        pupils += call(sum_kernel, [(each, points)], [], *received[h], after=before)
    results = []
    for h in range(halves):
        pieces = exchange([pupils[h]] * n_layer, "layer")[::-1]
        partial = call(
            functools.partial(fit_kernel, n_layer, n_row),
            [(chunk // halves, actuators)] * n_row,
            [pltpu.VMEM((n_layer, each, points), BF16), pltpu.VMEM((per_half, actuators), F32)],
            fitting.T,
            *pieces,
            after=pupils[h + 1 :],
        )
        results.append(exchange(partial, "row"))
    (out,) = call(finish_kernel, [(chunk, actuators)], [], *(part for got in results for part in got))
    return out


def solution(mesh):
    return jax.shard_map(
        local,
        mesh=mesh,
        in_specs=(
            P("layer", "row", "panel"),
            P(),
            P("row", "layer"),
            P("layer", "row", None),
            P("layer", "row"),
            P("layer", "row"),
            P("layer", "row"),
        ),
        out_specs=P(("panel", "row"), "layer"),
        check_vma=False,
    )
```

```python
import functools

import jax
import jax.numpy as jnp
from jax import lax
from jax.experimental import pallas as pl
from jax.experimental.pallas import tpu as pltpu
from jax.sharding import PartitionSpec as P

LANES = 128
CODE_ROWS = 16
F32, BF16 = jnp.float32, jnp.bfloat16
VMEM = pl.BlockSpec(memory_space=pltpu.VMEM)
ANY = pl.BlockSpec(memory_space=pl.ANY)
PARAMS = dict(vmem_limit_bytes=16 * 1024 * 1024)


def partners(n):
    return [0, n // 2] + [k for k in range(n - 1, 0, -1) if k != n // 2]


def turn_kernel(n_layer, n_row, halves, half, layers_ref, extra_ref, *refs):
    outs, codes = refs[:n_layer], refs[-1]
    rows_dev, columns = layers_ref.shape
    per_half = columns // halves
    each = per_half // n_layer
    chunk, part = columns // n_row, columns // n_row // halves
    me = lax.axis_index("layer")
    row = lax.broadcasted_iota(jnp.int32, (per_half, columns), 0)
    col = lax.broadcasted_iota(jnp.int32, (per_half, columns), 1)
    place = lax.bitwise_xor(row // each, me) * each + lax.rem(row, each)
    wanted = (place // part) * chunk + lax.rem(place, part) + half * part
    pick = (col == wanted).astype(BF16)
    turned = lax.dot_general(
        pick, layers_ref[...], (((1,), (1,)), ((), ())), preferred_element_type=F32
    ).astype(BF16)
    for i, out in enumerate(outs):
        k = partners(n_layer)[i]
        out[:, :rows_dev] = turned[k * each : (k + 1) * each]
    if half == 0:
        codes[...] = jnp.zeros_like(codes)
        codes[: extra_ref.shape[0], : extra_ref.shape[1]] = extra_ref[...]
        tail = codes[...].astype(F32).astype(BF16)
        for out in outs:
            out[:, rows_dev:] = jnp.zeros((each, LANES), BF16)
            out[:CODE_ROWS, rows_dev:] = tail


def pad_kernel(table_ref, padded):
    weights, block_rows = table_ref.shape[:2]
    padded[...] = jnp.zeros_like(padded)
    for half in range(LANES // block_rows):
        start = half * block_rows
        padded[half * weights : (half + 1) * weights, start : start + block_rows] = table_ref[...]


def pupil_kernel(n_layer, n_row, entries, unroll, padded, *refs):
    coded, parts = refs[:n_layer], refs[n_layer : 2 * n_layer]
    outs = refs[2 * n_layer : 2 * n_layer + n_row]
    total, codes, code, sem = refs[-4:]
    weights = padded.shape[0] // 2
    owned = outs[0].shape[1] // LANES
    for j, ref in enumerate(coded):
        tail = ref[:CODE_ROWS, ref.shape[1] - LANES :]
        codes[j * CODE_ROWS : (j + 1) * CODE_ROWS] = tail.astype(F32).astype(jnp.int32)
    copy = pltpu.make_async_copy(codes, code, sem)
    copy.start()
    total[...] = jnp.zeros_like(total)
    copy.wait()
    for j, part in enumerate(parts):
        base = j * CODE_ROWS

        def step(group, carry):
            terms = []
            for u in range(unroll):
                e = group * unroll + u
                block = code[base + 2, e]
                source = part[:, pl.ds(pl.multiple_of((block // 2) * LANES, LANES), LANES)]
                weight = padded[lax.rem(block, 2) * weights + code[base + 3, e]]
                dest = code[base, e] * owned + code[base + 1, e]
                terms.append((dest, jnp.dot(source, weight, preferred_element_type=F32)))
            for dest, term in terms:
                total[dest] += term
            return carry

        lax.fori_loop(0, entries // unroll, step, 0)
    me = lax.axis_index("row")
    for i, out in enumerate(outs):
        k = partners(n_row)[i]
        base = lax.bitwise_xor(me, k) * owned
        for s in range(owned):
            out[:, s * LANES : (s + 1) * LANES] = total[base + s].astype(BF16)


def sum_kernel(*refs):
    refs[-1][...] = sum(ref[...].astype(F32) for ref in refs[:-1]).astype(BF16)


def fit_kernel(n_layer, n_row, fitting_ref, *refs):
    pieces, outs = refs[:n_layer], refs[n_layer : n_layer + n_row]
    left, product = refs[-2], refs[-1]
    aligned = n_layer == n_row
    me, row = lax.axis_index("layer"), lax.axis_index("row")
    for j, piece in enumerate(pieces):
        place = lax.bitwise_xor(me, partners(n_layer)[n_layer - 1 - j])
        left[lax.bitwise_xor(place, row) if aligned else place] = piece[...]
    columns = left.shape[0] * left.shape[1]
    found = lax.dot_general(
        left[...].reshape(columns, left.shape[2]),
        fitting_ref[...],
        (((1,), (1,)), ((), ())),
        preferred_element_type=F32,
    )
    each = columns // n_row
    if aligned:
        for i, out in enumerate(outs):
            k = partners(n_row)[i]
            out[...] = found[k * each : (k + 1) * each].astype(BF16)
    else:
        product[...] = found
        for i, out in enumerate(outs):
            k = partners(n_row)[i]
            start = pl.multiple_of(lax.bitwise_xor(row, k) * each, each)
            out[...] = product[pl.ds(start, each), :].astype(BF16)


def trade(chunk, axis, k):
    return lax.ppermute(chunk, axis, [(j, j ^ k) for j in range(lax.axis_size(axis))])


def exchange(chunks, axis):
    n = len(chunks)
    return [trade(chunk, axis, partners(n)[i]) if i else chunk for i, chunk in enumerate(chunks)]


def total_of(parts):
    return sum(part.astype(F32) for part in parts).astype(BF16)


def call(kernel, shapes, scratch, *args, after=()):
    given = len(args)

    def body(*refs):
        kernel(*refs[:given], *refs[given + len(after) :])

    return pl.pallas_call(
        body,
        out_shape=[jax.ShapeDtypeStruct(shape, BF16) for shape in shapes],
        in_specs=[VMEM] * len(args) + [ANY] * len(after),
        out_specs=[VMEM] * len(shapes),
        scratch_shapes=scratch,
        compiler_params=pltpu.CompilerParams(**PARAMS),
    )(*args, *after)


def local(layers, table, fitting, owner, local_slice, block_index, weight_index):
    n_layer, n_row = lax.axis_size("layer"), lax.axis_size("row")
    rows_dev, columns = layers.shape[1:]
    entries = owner.shape[1]
    weights, slice_rows, block_rows = table.shape
    points, actuators = fitting.shape
    owned = points // slice_rows
    chunk = columns // n_row
    halves = 2 if chunk % 32 == 0 else 1
    per_half = columns // halves
    each = per_half // n_layer

    indices = jnp.concatenate([owner[:, :, 0], local_slice, block_index, weight_index], 0)
    parts, before = [], ()
    for h in range(halves):
        turned = call(
            functools.partial(turn_kernel, n_layer, n_row, halves, h),
            [(each, rows_dev + (LANES if h == 0 else 0))] * n_layer,
            [pltpu.VMEM((CODE_ROWS, LANES), jnp.int32)],
            layers[0],
            indices,
            after=before,
        )
        before = (turned[0],)
        if h == 0:
            (padded,) = call(
                pad_kernel,
                [(LANES // block_rows * weights, LANES, slice_rows)],
                [],
                jnp.swapaxes(table, 1, 2),
                after=before,
            )
        else:
            turned, parts[-1][1], padded = lax.optimization_barrier((turned, parts[-1][1], padded))
        parts.append(exchange(turned, "layer"))

    received, before = [], ()
    for h in range(halves):
        shares = call(
            functools.partial(pupil_kernel, n_layer, n_row, entries, entries),
            [(each, points)] * n_row,
            [
                pltpu.VMEM((n_row * owned, each, slice_rows), F32),
                pltpu.VMEM((n_layer * CODE_ROWS, LANES), jnp.int32),
                pltpu.SMEM((n_layer * CODE_ROWS, LANES), jnp.int32),
                pltpu.SemaphoreType.DMA,
            ],
            padded,
            *parts[0],
            *parts[h],
            after=before,
        )
        before = (shares[0],)
        if h > 0:
            shares, received[-1] = lax.optimization_barrier((shares, received[-1]))
        received.append(exchange(shares, "row"))
    pupils = []
    for h in range(halves):
        pupils += call(sum_kernel, [(each, points)], [], *received[h], after=before)
    results = []
    for h in range(halves):
        pieces = exchange([pupils[h]] * n_layer, "layer")[::-1]
        partial = call(
            functools.partial(fit_kernel, n_layer, n_row),
            [(chunk // halves, actuators)] * n_row,
            [pltpu.VMEM((n_layer, each, points), BF16), pltpu.VMEM((per_half, actuators), F32)],
            fitting.T,
            *pieces,
            after=pupils[h + 1 :],
        )
        results.append(exchange(partial, "row"))
    return jnp.concatenate([total_of(result) for result in results], 0)


def solution(mesh):
    return jax.shard_map(
        local,
        mesh=mesh,
        in_specs=(
            P("layer", "row", "panel"),
            P(),
            P("row", "layer"),
            P("layer", "row", None),
            P("layer", "row"),
            P("layer", "row"),
            P("layer", "row"),
        ),
        out_specs=P(("panel", "row"), "layer"),
        check_vma=False,
    )
```

```python
import functools

import jax
import jax.numpy as jnp
from jax import lax
from jax.experimental import pallas as pl
from jax.experimental.pallas import tpu as pltpu
from jax.sharding import PartitionSpec as P

LANES = 128
CODE_ROWS = 16
F32, BF16 = jnp.float32, jnp.bfloat16
VMEM = pl.BlockSpec(memory_space=pltpu.VMEM)
ANY = pl.BlockSpec(memory_space=pl.ANY)
PARAMS = dict(vmem_limit_bytes=24 * 1024 * 1024)


def turn_kernel(n_layer, n_row, halves, half, layers_ref, extra_ref, *refs):
    outs, codes = refs[:n_layer], refs[-1]
    rows_dev, columns = layers_ref.shape
    per_half = columns // halves
    each = per_half // n_layer
    chunk, part = columns // n_row, columns // n_row // halves
    me = lax.axis_index("layer")
    row = lax.broadcasted_iota(jnp.int32, (per_half, columns), 0)
    col = lax.broadcasted_iota(jnp.int32, (per_half, columns), 1)
    place = lax.bitwise_xor(row // each, me) * each + lax.rem(row, each)
    wanted = (place // part) * chunk + lax.rem(place, part) + half * part
    pick = (col == wanted).astype(BF16)
    turned = lax.dot_general(
        pick, layers_ref[...], (((1,), (1,)), ((), ())), preferred_element_type=F32
    ).astype(BF16)
    for i, out in enumerate(outs):
        k = (n_layer - i) % n_layer
        out[:, :rows_dev] = turned[k * each : (k + 1) * each]
    if half == 0:
        codes[...] = jnp.zeros_like(codes)
        codes[: extra_ref.shape[0], : extra_ref.shape[1]] = extra_ref[...]
        tail = codes[...].astype(F32).astype(BF16)
        for out in outs:
            out[:, rows_dev:] = jnp.zeros((each, LANES), BF16)
            out[:CODE_ROWS, rows_dev:] = tail


def pad_kernel(table_ref, padded):
    weights, block_rows = table_ref.shape[:2]
    padded[...] = jnp.zeros_like(padded)
    for half in range(LANES // block_rows):
        start = half * block_rows
        padded[half * weights : (half + 1) * weights, start : start + block_rows] = table_ref[...]


def pupil_kernel(n_layer, n_row, entries, unroll, padded, *refs):
    coded, parts = refs[:n_layer], refs[n_layer : 2 * n_layer]
    outs = refs[2 * n_layer : 2 * n_layer + n_row]
    totals, (codes, code, sem) = refs[-5:-3], refs[-3:]
    weights = padded.shape[0] // 2
    owned = outs[0].shape[1] // LANES
    for j, ref in enumerate(coded):
        tail = ref[:CODE_ROWS, ref.shape[1] - LANES :]
        codes[j * CODE_ROWS : (j + 1) * CODE_ROWS] = tail.astype(F32).astype(jnp.int32)
    copy = pltpu.make_async_copy(codes, code, sem)
    copy.start()
    for total in totals:
        total[...] = jnp.zeros_like(total)
    copy.wait()
    for j, part in enumerate(parts):
        base = j * CODE_ROWS

        def step(group, carry):
            terms = []
            for u in range(unroll):
                e = group * unroll + u
                block = code[base + 2, e]
                source = part[:, pl.ds(pl.multiple_of((block // 2) * LANES, LANES), LANES)]
                weight = padded[lax.rem(block, 2) * weights + code[base + 3, e]]
                dest = code[base, e] * owned + code[base + 1, e]
                terms.append((dest, jnp.dot(source, weight, preferred_element_type=F32)))
            for i, (dest, term) in enumerate(terms):
                totals[i % 2][dest] += term
            return carry

        lax.fori_loop(0, entries // unroll, step, 0)
    me = lax.axis_index("row")
    for i, out in enumerate(outs):
        k = (n_row - i) % n_row
        base = lax.bitwise_xor(me, k) * owned
        for s in range(owned):
            out[:, s * LANES : (s + 1) * LANES] = (totals[0][base + s] + totals[1][base + s]).astype(BF16)


def sum_kernel(*refs):
    refs[-1][...] = sum(ref[...].astype(F32) for ref in refs[:-1]).astype(BF16)


def fit_kernel(n_layer, n_row, fitting_ref, *refs):
    pieces, outs = refs[:n_layer], refs[n_layer : n_layer + n_row]
    left, product = refs[-2], refs[-1]
    aligned = n_layer == n_row
    me, row = lax.axis_index("layer"), lax.axis_index("row")
    for j, piece in enumerate(pieces):
        place = lax.bitwise_xor(me, (j + 1) % n_layer)
        left[lax.bitwise_xor(place, row) if aligned else place] = piece[...]
    columns = left.shape[0] * left.shape[1]
    found = lax.dot_general(
        left[...].reshape(columns, left.shape[2]),
        fitting_ref[...],
        (((1,), (1,)), ((), ())),
        preferred_element_type=F32,
    )
    each = columns // n_row
    if aligned:
        for i, out in enumerate(outs):
            k = (n_row - i) % n_row
            out[...] = found[k * each : (k + 1) * each].astype(BF16)
    else:
        product[...] = found
        for i, out in enumerate(outs):
            k = (n_row - i) % n_row
            start = pl.multiple_of(lax.bitwise_xor(row, k) * each, each)
            out[...] = product[pl.ds(start, each), :].astype(BF16)


def trade(chunk, axis, k):
    return lax.ppermute(chunk, axis, [(j, j ^ k) for j in range(lax.axis_size(axis))])


def exchange(chunks, axis):
    n = len(chunks)
    return [trade(chunk, axis, n - i) if i else chunk for i, chunk in enumerate(chunks)]


def total_of(parts):
    return sum(part.astype(F32) for part in parts).astype(BF16)


def call(kernel, shapes, scratch, *args, after=()):
    given = len(args)

    def body(*refs):
        kernel(*refs[:given], *refs[given + len(after) :])

    return pl.pallas_call(
        body,
        out_shape=[jax.ShapeDtypeStruct(shape, BF16) for shape in shapes],
        in_specs=[VMEM] * len(args) + [ANY] * len(after),
        out_specs=[VMEM] * len(shapes),
        scratch_shapes=scratch,
        compiler_params=pltpu.CompilerParams(**PARAMS),
    )(*args, *after)


def local(layers, table, fitting, owner, local_slice, block_index, weight_index):
    n_layer, n_row = lax.axis_size("layer"), lax.axis_size("row")
    rows_dev, columns = layers.shape[1:]
    entries = owner.shape[1]
    weights, slice_rows, block_rows = table.shape
    points, actuators = fitting.shape
    owned = points // slice_rows
    chunk = columns // n_row
    halves = 2 if chunk % 32 == 0 else 1
    per_half = columns // halves
    each = per_half // n_layer

    indices = jnp.concatenate([owner[:, :, 0], local_slice, block_index, weight_index], 0)
    parts, before = [], ()
    for h in range(halves):
        turned = call(
            functools.partial(turn_kernel, n_layer, n_row, halves, h),
            [(each, rows_dev + (LANES if h == 0 else 0))] * n_layer,
            [pltpu.VMEM((CODE_ROWS, LANES), jnp.int32)],
            layers[0],
            indices,
            after=before,
        )
        before = (turned[0],)
        if h == 0:
            (padded,) = call(
                pad_kernel,
                [(LANES // block_rows * weights, LANES, slice_rows)],
                [],
                jnp.swapaxes(table, 1, 2),
                after=before,
            )
        else:
            turned, parts[-1][1], padded = lax.optimization_barrier((turned, parts[-1][1], padded))
        parts.append(exchange(turned, "layer"))

    received, before = [], ()
    for h in range(halves):
        shares = call(
            functools.partial(pupil_kernel, n_layer, n_row, entries, entries),
            [(each, points)] * n_row,
            [
                pltpu.VMEM((n_row * owned, each, slice_rows), F32),
                pltpu.VMEM((n_row * owned, each, slice_rows), F32),
                pltpu.VMEM((n_layer * CODE_ROWS, LANES), jnp.int32),
                pltpu.SMEM((n_layer * CODE_ROWS, LANES), jnp.int32),
                pltpu.SemaphoreType.DMA,
            ],
            padded,
            *parts[0],
            *parts[h],
            after=before,
        )
        before = (shares[0],)
        if h > 0:
            shares, received[-1] = lax.optimization_barrier((shares, received[-1]))
        received.append(exchange(shares, "row"))
    pupils = []
    for h in range(halves):
        pupils += call(sum_kernel, [(each, points)], [], *received[h], after=before)
    results = []
    for h in range(halves):
        pieces = exchange([pupils[h]] * n_layer, "layer")[::-1]
        partial = call(
            functools.partial(fit_kernel, n_layer, n_row),
            [(chunk // halves, actuators)] * n_row,
            [pltpu.VMEM((n_layer, each, points), BF16), pltpu.VMEM((per_half, actuators), F32)],
            fitting.T,
            *pieces,
            after=pupils[h + 1 :],
        )
        results.append(exchange(partial, "row"))
    return jnp.concatenate([total_of(result) for result in results], 0)


def solution(mesh):
    return jax.shard_map(
        local,
        mesh=mesh,
        in_specs=(
            P("layer", "row", "panel"),
            P(),
            P("row", "layer"),
            P("layer", "row", None),
            P("layer", "row"),
            P("layer", "row"),
            P("layer", "row"),
        ),
        out_specs=P(("panel", "row"), "layer"),
        check_vma=False,
    )
```
